128 devices in a mesh: gx: 8 (over x, core), gy: 16 (over y, z).
Axes of the slice: x: 4, y: 4, z: 4, core: 2. Of those that a mesh axis runs over, the one named last changes fastest.
Arguments:
- blocks: float32 [16, 16, 9, 128, 128], P('gx', 'gy'), may hold values from -0.0625 to 0.0625
- pair_mask: int32 [16, 16, 9, 8, 8], P('gx', 'gy'), may hold values 0 or 1
- rhs_rows: float32 [16, 16, 9, 128, 128], P('gx', 'gy'), may hold values from -6 to 6
- counts: int32 [16, 16, 8], P('gx', 'gy'), may hold values from 1 to 3, as said below
Outputs:
- solution: float32 [16, 16, 9, 128, 128], P('gx', 'gy')
The draws below stay inside these ranges and needn't reach their ends.
Inputs may be any that keep to these rules, and one draw needn't show every extreme that they name: `counts`: cut the first block index into runs of 2 blocks. Within each second index b, run a and run a + 4 together hold at most 2 blocks that have an atom with a count of 2 or more, and some run holds 2 such blocks; at least one atom takes 3 iterations and at least one takes 1.
All inputs are finite; a program needn't handle non-finite values. No bound on the sum of `pair_mask` on one device may be relied on, other than what follows from the above.
Results may differ from the reference program's by a relative error of at most 0.0003.
Values sent between devices are 32-bit elements; how exact they have to be, the bound alone decides.
No kernel may reach another device: no remote copies, remote signals or barrier semaphores. Data moves between devices by JAX's collectives and lax.ppermute only.
A program may use at most 128 MiB of HBM per device.

```python
import jax
import jax.numpy as jnp
from jax import lax

ORB = 16
ATOMS = 8
B = 128
OFFSETS = 9
GRP_X = 2
ITERS = 3
NGX = 16
NGY = 16


def draw_counts(key, part):
    groups = NGX // GRP_X
    half_groups = groups // 2
    pair_count = half_groups * NGY
    key_total = jax.random.fold_in(key, 21)
    key_split = jax.random.fold_in(key, 22)
    key_forced = jax.random.fold_in(key, 23)
    key_scores = jax.random.fold_in(key, 24)
    key_base = jax.random.fold_in(key, 25)
    key_leading = jax.random.fold_in(key, 26)
    key_lead_val = jax.random.fold_in(key, 27)
    totals = jax.random.randint(key_total, (pair_count,), 0, GRP_X + 1, dtype=jnp.int32)
    lower = jax.random.randint(key_split, (pair_count,), 0, totals + 1, dtype=jnp.int32)
    forced = jax.random.randint(key_forced, (), 0, pair_count, dtype=jnp.int32)
    pair_ids = jnp.arange(pair_count, dtype=jnp.int32)
    totals = jnp.where(pair_ids == forced, GRP_X, totals)
    lower = jnp.where(pair_ids == forced, GRP_X, lower)
    upper = totals - lower
    loads = jnp.concatenate([lower.reshape(half_groups, NGY), upper.reshape(half_groups, NGY)], axis=0)
    local_ids = jnp.arange(GRP_X, dtype=jnp.int32)
    scores = jax.random.randint(key_scores, (groups, NGY, GRP_X), 0, 1 << 20, dtype=jnp.int32) * GRP_X + local_ids
    ranks = jnp.argsort(jnp.argsort(scores, axis=-1), axis=-1).astype(jnp.int32)
    slow = ranks < loads[..., None]
    base_counts = jax.random.randint(key_base, (groups, NGY, GRP_X, ATOMS), 1, 4, dtype=jnp.int32)
    leading = jax.random.randint(key_leading, (groups, NGY, GRP_X), 0, ATOMS, dtype=jnp.int32)
    lead_val = jax.random.randint(key_lead_val, (groups, NGY, GRP_X), 2, 4, dtype=jnp.int32)
    group_ids = jnp.arange(groups, dtype=jnp.int32)[:, None, None]
    column_ids = jnp.arange(NGY, dtype=jnp.int32)[None, :, None]
    forced_device = (group_ids == forced // NGY) & (column_ids == forced % NGY) & (ranks == 0)
    lead_val = jnp.where(forced_device, ITERS, lead_val)
    atom_ids = jnp.arange(ATOMS, dtype=jnp.int32)
    atom_counts = jnp.where(atom_ids == leading[..., None], lead_val[..., None], base_counts)
    result = jnp.where(slow[..., None], atom_counts, 1)
    result = jnp.transpose(result, (0, 2, 1, 3)).reshape(NGX, NGY, ATOMS)
    return result.astype(jnp.int32)


def touch_ends(values, rng, least, largest):
    spot = [jax.random.randint(jax.random.fold_in(rng, axis), (), 0, length) for axis, length in enumerate(values.shape)]
    widest = values.shape.index(max(values.shape))
    neighbour = spot[:widest] + [(spot[widest] + 1) % values.shape[widest]] + spot[widest + 1:]
    return values.at[tuple(spot)].set(least).at[tuple(neighbour)].set(largest)


def steps_of(rng, shape, split, low, top_value):
    gain, own = 1.0, jax.random.fold_in(rng, 6)
    for dim, parts in split:
        draws = jnp.exp(jax.random.uniform(jax.random.fold_in(own, dim), (parts,), jnp.float32, low / len(split), top_value / len(split)))
        gain = gain * jnp.repeat(draws, shape[dim] // parts).reshape([-1 if axis == dim else 1 for axis in range(len(shape))])
    return gain


def normal_values(own_key, extent, deviation, bound, cuts=(), held_as=jnp.bfloat16):
    array = jax.random.normal(own_key, extent, jnp.float32) * deviation
    if len(cuts) > 0:
        array = steps_of(own_key, extent, cuts, -0.22, 0.18) * array
    return jnp.clip(array, min=-bound, max=bound).astype(held_as)


def setup_inputs(seed: int = 0) -> dict:
    seeds = jax.random.split(jax.random.key(seed), 5)
    blocks = normal_values(seeds[0], (NGX, NGY, OFFSETS, B, B), (81 * B) ** -0.5, 0.0625, ((0, 8), (1, 16)), jnp.float32)
    pair_mask = touch_ends((jax.random.randint(seeds[1], (NGX, NGY, OFFSETS, ATOMS, ATOMS), 0, 4) < 3).astype(jnp.int32), jax.random.fold_in(seeds[1], 1), 0, 1)
    rhs_rows = normal_values(seeds[2], (NGX, NGY, OFFSETS, B, B), 1.0, 6.0, ((0, 8), (1, 16)), jnp.float32)
    counts = draw_counts(jax.random.fold_in(seeds[4], 71), 0)
    return dict(blocks=blocks, pair_mask=pair_mask, rhs_rows=rhs_rows, counts=counts)


def expand_mask(pair_mask, orbitals):
    shaped = pair_mask.astype(jnp.float32)[..., :, None, :, None]
    leading = pair_mask.shape[:-2]
    atom_count = pair_mask.shape[-1]
    expanded = jnp.broadcast_to(shaped, leading + (atom_count, orbitals, atom_count, orbitals))
    return expanded.reshape(leading + (atom_count * orbitals, atom_count * orbitals))

def cluster_apply(window, vectors):
    result = vectors
    for row_off in (-1, 0, 1):
        for col_off in (-1, 0, 1):
            offset = 3 * (row_off + 1) + (col_off + 1)
            row_low, row_high = (max(0, -row_off), min(3, 3 - row_off))
            col_low, col_high = (max(0, -col_off), min(3, 3 - col_off))
            coupled = window[..., row_low:row_high, col_low:col_high, offset, :, :]
            source = vectors[..., row_low + row_off:row_high + row_off, col_low + col_off:col_high + col_off, :, :]
            product = jnp.einsum('...xyij,...xyjc->...xyic', coupled, source, precision=lax.Precision.HIGHEST)
            result = result.at[..., row_low:row_high, col_low:col_high, :, :].add(-product)
    return result

def cluster_rhs(rhs_window):
    rows_list = []
    for row_pos in range(3):
        pieces = []
        for col_pos in range(3):
            pieces.append(rhs_window[..., row_pos, col_pos, 8 - 3 * row_pos - col_pos, :, :])
        rows_list.append(jnp.stack(pieces, axis=-3))
    return jnp.stack(rows_list, axis=-4)

def column_inner(left, other):
    return lax.optimization_barrier(jnp.sum(left * other, axis=(-4, -3, -2)))

def spread(scalar):
    return scalar[..., None, None, None, :]

def guarded(top, bottom, floor_val):
    return top * bottom / (bottom * bottom + floor_val * floor_val)

def start_state(window, right_side):
    image_first = cluster_apply(window, right_side)
    zero_field = jnp.zeros_like(right_side)
    norm_rhs = column_inner(right_side, right_side)
    zero_cols = jnp.zeros_like(norm_rhs)
    vectors = (right_side, right_side, right_side, image_first, image_first, zero_field, zero_field)
    scalars = (norm_rhs, 0.1 * norm_rhs, jnp.sqrt(norm_rhs), zero_cols, zero_cols, norm_rhs)
    return (vectors, scalars)

def iterate(window, vectors, scalars, iteration, limit_cols):
    shadow, residual, first_dir, image_first, vector, direction, solution = vectors
    rho_value, rho_floor, tau_value, theta_value, eta_value, norm_rhs = scalars
    alpha_floor = 0.1 * jnp.sqrt(norm_rhs * (column_inner(vector, vector) + 1e-06))
    alpha_value = guarded(rho_value, column_inner(shadow, vector), alpha_floor)
    step_ratio = guarded(1.0, alpha_value, 0.1)
    second = first_dir - spread(alpha_value) * vector
    image_second = cluster_apply(window, second)
    active = spread((limit_cols > iteration).astype(jnp.float32))
    for half_dir, half_image in ((first_dir, image_first), (second, image_second)):
        residual = residual - spread(alpha_value) * half_image
        direction = half_dir + spread(theta_value * theta_value * eta_value * step_ratio) * direction
        theta_value = jnp.sqrt(column_inner(residual, residual)) / tau_value
        cosine = 1.0 / jnp.sqrt(1.0 + theta_value * theta_value)
        tau_value = tau_value * theta_value * cosine
        eta_value = cosine * cosine * alpha_value
        solution = solution + active * spread(eta_value) * direction
    vectors = (shadow, residual, second, image_second, vector, direction, solution)
    scalars = (rho_value, rho_floor, tau_value, theta_value, eta_value, norm_rhs)
    return (vectors, scalars)

def advance(window, vectors, scalars):
    shadow, residual, second, image_second, vector, direction, solution = vectors
    rho_value, rho_floor, tau_value, theta_value, eta_value, norm_rhs = scalars
    rho_next = column_inner(shadow, residual)
    beta_value = guarded(rho_next, rho_value, rho_floor)
    next_floor = 0.1 * jnp.sqrt(norm_rhs * column_inner(residual, residual))
    first_dir = residual + spread(beta_value) * second
    image_first = cluster_apply(window, first_dir)
    vector = image_first + spread(beta_value) * (image_second + spread(beta_value) * vector)
    vectors = (shadow, residual, first_dir, image_first, vector, direction, solution)
    scalars = (rho_next, next_floor, tau_value, theta_value, eta_value, norm_rhs)
    return (vectors, scalars)

def first_section(window, right_side, limit_cols):
    vectors, scalars = start_state(window, right_side)
    return iterate(window, vectors, scalars, 0, limit_cols)

def later_section(window, vectors, scalars, limit_cols):
    for iteration in range(1, ITERS):
        vectors, scalars = advance(window, vectors, scalars)
        vectors, scalars = iterate(window, vectors, scalars, iteration, limit_cols)
    return vectors[6]

def reference(blocks, pair_mask, rhs_rows, counts):
    coupling = blocks * expand_mask(pair_mask, ORB)
    widths = ((1, 1), (1, 1), (0, 0), (0, 0), (0, 0))
    padded_coupling = jnp.pad(coupling, widths)
    padded_rhs = jnp.pad(rhs_rows, widths)
    limits = jnp.repeat(counts, ORB, axis=-1).astype(jnp.float32)

    def one_group(block_index):
        zero_idx = jnp.zeros((), jnp.int32)
        first_pos = (block_index // NGY).astype(jnp.int32)
        second_pos = (block_index % NGY).astype(jnp.int32)
        starts = (first_pos, second_pos, zero_idx, zero_idx, zero_idx)
        window = lax.dynamic_slice(padded_coupling, starts, (3, 3, OFFSETS, B, B))
        rhs_window = lax.dynamic_slice(padded_rhs, starts, (3, 3, OFFSETS, B, B))
        limit_cols = lax.dynamic_slice(limits, (first_pos, second_pos, zero_idx), (1, 1, B)).reshape(B)
        vectors, scalars = first_section(window, cluster_rhs(rhs_window), limit_cols)
        return later_section(window, vectors, scalars, limit_cols)
    result = lax.map(one_group, jnp.arange(NGX * NGY, dtype=jnp.int32))
    return result.reshape(NGX, NGY, OFFSETS, B, B)
```

```python
import jax
import jax.numpy as jnp
from jax import lax
from jax.experimental import pallas as pl
from jax.experimental.pallas import tpu as pltpu
from jax.sharding import PartitionSpec as P

ITERS = 3
B = 128
POWERS = 2 * ITERS + 1
F32 = jnp.float32
BF16 = jnp.bfloat16


def off(u, v):
    return 3 * (u + 1) + (v + 1)


def edge_list(v):
    low, high = min(0, v), max(0, v)
    first = []
    for row, us in ((0, (-1, 0)), (1, (0, 1))):
        first += [(row, True, off(u, w)) for u in us for w in (low, high)]
        first.append((row, False, off(-1 if row == 0 else 1, v)))
    second = []
    for row, u in ((0, 1), (1, -1)):
        second += [(row, True, off(u, w)) for w in (low, high)]
        second += [(row, False, off(0, v)), (row, False, off(u, v))]
    return first, second


def own_list(u):
    row, us = (1, (0, 1)) if u > 0 else (0, (-1, 0))
    return [(row, True, off(w, v)) for w in us for v in (-1, 0, 1)] + [(row, False, off(u, 0))]


FIRST = {v: edge_list(v)[0] for v in (1, -1)}
SECOND = {v: edge_list(v)[1] for v in (1, -1)}
OWN = {u: own_list(u) for u in (1, -1)}


def pack_kernel(blocks, mask, rhs, sap, sam, sbp, sbm, oxp, oxm, own):
    atoms = mask.shape[-1]
    orbitals = B // atoms
    lane_atom = lax.broadcasted_iota(jnp.int32, (atoms, B), 1) // orbitals
    atom = lax.broadcasted_iota(jnp.int32, (atoms, B), 0)
    spread = (lane_atom == atom).astype(BF16)
    flat = mask[...].reshape(18 * atoms, atoms).astype(F32).astype(BF16)
    wide = jnp.dot(flat, spread, preferred_element_type=F32)
    masked = {}
    for row in range(2):
        for o in range(9):
            start = (row * 9 + o) * atoms
            rows = [
                jnp.broadcast_to(wide[start + a : start + a + 1, :], (orbitals, B))
                for a in range(atoms)
            ]
            own[row, o] = blocks[row, 0, o] * jnp.concatenate(rows, axis=0)
    for ref, entries in (
        (sap, FIRST[1]),
        (sam, FIRST[-1]),
        (sbp, SECOND[1]),
        (sbm, SECOND[-1]),
        (oxp, OWN[1]),
        (oxm, OWN[-1]),
    ):
        for place, (row, is_coupling, o) in enumerate(entries):
            ref[place] = own[row, o] if is_coupling else rhs[row, 0, o]


def pack(blocks, mask, rhs):
    shapes = [10, 10, 8, 8, 7, 7]
    out = [jax.ShapeDtypeStruct((n, B, B), F32) for n in shapes]
    out.append(jax.ShapeDtypeStruct((2, 9, B, B), F32))
    return pl.pallas_call(
        pack_kernel,
        out_shape=out,
        in_specs=[pl.BlockSpec(memory_space=pltpu.VMEM)] * 3,
        out_specs=[pl.BlockSpec(memory_space=pltpu.VMEM)] * 7,
        compiler_params=pltpu.CompilerParams(vmem_limit_bytes=32 * 2**20),
        name="pack",
    )(blocks, mask, rhs)


def split(value):
    high = value.astype(BF16)
    low = (value - high.astype(F32)).astype(BF16)
    return high, low


def guarded(top, bottom, floor_val):
    return top * bottom / (bottom * bottom + floor_val * floor_val)


def poly_add(left, scale, right):
    out = []
    for i in range(max(len(left), len(right))):
        if i >= len(right):
            out.append(left[i])
        elif i >= len(left):
            out.append(scale * right[i])
        else:
            out.append(left[i] + scale * right[i])
    return out


def poly_apply(p):
    return poly_add(list(p), -1.0, [jnp.zeros_like(p[0])] + list(p))


def poly_first(gram, p):
    total = p[0] * gram[0][0]
    for i in range(1, len(p)):
        total = total + p[i] * gram[0][i]
    return total


def poly_norm(gram, p):
    total = 0.0
    for i in range(len(p)):
        inner = p[i] * gram[i][i]
        for j in range(i):
            inner = inner + 2.0 * (p[j] * gram[j][i])
        total = total + p[i] * inner
    return total


def tfqmr(gram, limits):
    one = jnp.ones_like(limits)
    zero = jnp.zeros_like(limits)
    norm = gram[0][0]
    w = [one]
    y1 = [one]
    u1 = poly_apply(y1)
    v = u1
    d = [zero]
    x = [zero]
    rho, floor_val, tau = norm, 0.1 * norm, jnp.sqrt(norm)
    theta = zero
    eta = zero
    y2 = None
    u2 = None
    ww = norm
    for iteration in range(ITERS):
        if iteration > 0:
            rho_next = poly_first(gram, w)
            beta = guarded(rho_next, rho, floor_val)
            floor_val = 0.1 * jnp.sqrt(norm * ww)
            rho = rho_next
            y1 = poly_add(w, beta, y2)
            u1 = poly_apply(y1)
            v = poly_add(u1, beta, poly_add(u2, beta, v))
        alpha_floor = 0.1 * jnp.sqrt(norm * (poly_norm(gram, v) + 1e-06))
        alpha = guarded(rho, poly_first(gram, v), alpha_floor)
        ratio = guarded(1.0, alpha, 0.1)
        y2 = poly_add(y1, -alpha, v)
        u2 = poly_apply(y2)
        active = (limits > iteration).astype(F32)
        for y, u in ((y1, u1), (y2, u2)):
            w = poly_add(w, -alpha, u)
            d = poly_add(y, theta * theta * eta * ratio, d)
            ww = poly_norm(gram, w)
            theta = jnp.sqrt(ww) / tau
            cosine = 1.0 / jnp.sqrt(1.0 + theta * theta)
            tau = tau * theta * cosine
            eta = cosine * cosine * alpha
            x = poly_add(x, active * eta, d)
    return x


def column_range(c):
    return (0, 2) if c == 0 else (0, 3) if c == 1 else (1, 3)


def solve_kernel(
    rap, ram, rbp, rbm, rxp, rxm, fxp, fxm, own, rhs, limits, out, wh, wl, vv, powers, gram_ref
):
    def put_coupling(h, c, o, value):
        high, low = split(value)
        wh[h, c, :, o * B : (o + 1) * B] = high
        wl[h, c, :, o * B : (o + 1) * B] = low

    def put_vector(slot, parity, g, r, c, value):
        high, low = split(value)
        start = ((g + r) * 3 + c) * B
        vv[parity, start : start + B, g * B : (g + 1) * B] = high
        vv[parity, start : start + B, (2 + g) * B : (3 + g) * B] = low
        powers[slot, g, (3 * r + c) * B : (3 * r + c + 1) * B, :] = value

    def put_rhs(h, c, o, value):
        r = 1 - (o // 3 - 1)
        g = h - r
        put_vector(0, 0, g, r, c, value)

    for v, ref_a, ref_b in ((1, rap, rbp), (-1, ram, rbm)):
        c = 1 - v
        for ref, entries in ((ref_a, FIRST[v]), (ref_b, SECOND[v])):
            for place, (row, is_coupling, o) in enumerate(entries):
                if is_coupling:
                    put_coupling(row + 1, c, o, ref[place])
                elif 0 <= row + (o // 3 - 1) <= 1:
                    put_rhs(row + 1, c, o, ref[place])
    for u, ref, fref in ((1, rxp, fxp), (-1, rxm, fxm)):
        h = 0 if u > 0 else 3
        for place, (row, is_coupling, o) in enumerate(OWN[u]):
            if is_coupling:
                put_coupling(h, 1, o, ref[place])
            else:
                put_rhs(h, 1, o, ref[place])
        part = 5 if u > 0 else 0
        for side, v in ((0, 1), (1, -1)):
            for place in range(5):
                row, is_coupling, o = FIRST[v][part + place]
                if is_coupling:
                    put_coupling(h, 1 - v, o, fref[side * 5 + place])
                else:
                    put_rhs(h, 1 - v, o, fref[side * 5 + place])
    for row in range(2):
        for o in range(9):
            put_coupling(row + 1, 1, o, own[row, o])
    for row, u in ((0, 0), (1, 0), (0, 1), (1, -1)):
        put_rhs(row + 1, 1, off(u, 0), rhs[row, 0, off(u, 0)])

    def dot(left, right):
        return jnp.dot(left, right, preferred_element_type=F32)

    def piece(h, c, source_low, source_high, parity, lanes):
        c_low, c_high = column_range(c)
        runs = []
        if c == 1:
            runs.append((source_low * 3, off(source_low - h, -1), 3 * (source_high - source_low)))
        else:
            for source in range(source_low, source_high):
                runs.append((source * 3 + c_low, off(source - h, c_low - c), 2))
        both = None
        for member, o, count in runs:
            left_h = wh[h, c, :, o * B : (o + count) * B]
            left_l = wl[h, c, :, o * B : (o + count) * B]
            rows = slice(member * B, (member + count) * B)
            if lanes is None:
                high = dot(left_h, vv[parity, rows, :])
                low = dot(left_l, vv[parity, rows, : 2 * B])
                term = (
                    high[:, :B] + (high[:, 2 * B : 3 * B] + low[:, :B]),
                    high[:, B : 2 * B] + (high[:, 3 * B :] + low[:, B:]),
                )
            else:
                g = lanes
                right_h = vv[parity, rows, g * B : (g + 1) * B]
                right_l = vv[parity, rows, (2 + g) * B : (3 + g) * B]
                high = dot(left_h, jnp.concatenate([right_h, right_l], axis=1))
                low = dot(left_l, right_h)
                term = (high[:, :B] + (high[:, B:] + low),)
            both = term if both is None else tuple(a + b for a, b in zip(both, term))
        return both

    def apply(slot, parity):
        for c in range(3):
            for h in (1, 2):
                shared = piece(h, c, 1, 3, parity, None)
                g = h - 1
                extra = piece(h, c, 0, 1, parity, 0) if h == 1 else piece(h, c, 3, 4, parity, 1)
                values = [shared[0], shared[1]]
                values[g] = values[g] + extra[0]
                for group in range(2):
                    put_vector(slot + 1, 1 - parity, group, h - group, c, values[group])
            put_vector(slot + 1, 1 - parity, 0, 0, c, piece(0, c, 0, 2, parity, 0)[0])
            put_vector(slot + 1, 1 - parity, 1, 2, c, piece(3, c, 2, 4, parity, 1)[0])

    def grams(slot):
        for g in range(2):
            totals = [None] * POWERS
            for m in range(9):
                rows = slice(m * B, (m + 1) * B)
                here = powers[slot, g, rows, :]
                for i in range(POWERS):
                    term = jnp.sum((here * powers[i, g, rows, :]).reshape(16, 8, B), axis=0)
                    totals[i] = term if totals[i] is None else totals[i] + term
            for i in range(POWERS):
                gram_ref[slot, i, g] = totals[i]

    def body(slot, carry):
        grams(slot)
        apply(slot, lax.rem(slot, 2))
        return carry

    lax.fori_loop(0, POWERS - 1, body, 0)
    grams(POWERS - 1)
    gram = [
        [
            jnp.concatenate(
                [jnp.sum(gram_ref[max(i, j), min(i, j), g], axis=0, keepdims=True) for g in range(2)],
                axis=0,
            )
            for j in range(POWERS)
        ]
        for i in range(POWERS)
    ]
    x = tfqmr(gram, limits[...])
    for g in range(2):
        for m in range(9):
            rows = slice(m * B, (m + 1) * B)
            total = x[0][g : g + 1, :] * powers[0, g, rows, :]
            for i in range(1, len(x)):
                total = total + x[i][g : g + 1, :] * powers[i, g, rows, :]
            out[g, 0, m] = total


def solve(*arrays):
    return pl.pallas_call(
        solve_kernel,
        out_shape=jax.ShapeDtypeStruct((2, 1, 9, B, B), F32),
        in_specs=[pl.BlockSpec(memory_space=pltpu.VMEM)] * len(arrays),
        out_specs=pl.BlockSpec(memory_space=pltpu.VMEM),
        scratch_shapes=[
            pltpu.VMEM((4, 3, B, 9 * B), BF16),
            pltpu.VMEM((4, 3, B, 9 * B), BF16),
            pltpu.VMEM((2, 12 * B, 4 * B), BF16),
            pltpu.VMEM((POWERS, 2, 9 * B, B), F32),
            pltpu.VMEM((POWERS, POWERS, 2, 8, B), F32),
        ],
        compiler_params=pltpu.CompilerParams(vmem_limit_bytes=32 * 2**20),
        name="solve",
    )(*arrays)


def shift(value, axis, step):
    count = lax.axis_size(axis)
    if step > 0:
        pairs = [(i, i + 1) for i in range(count - 1)]
    else:
        pairs = [(i + 1, i) for i in range(count - 1)]
    return lax.ppermute(value, axis, pairs)


def shards(blocks, pair_mask, rhs_rows, counts):
    sap, sam, sbp, sbm, oxp, oxm, own = pack(blocks, pair_mask, rhs_rows)
    rap = shift(sap, "gy", 1)
    ram = shift(sam, "gy", -1)
    rxp = shift(oxp, "gx", 1)
    rxm = shift(oxm, "gx", -1)
    rbp = shift(sbp, "gy", 1)
    rbm = shift(sbm, "gy", -1)
    fxp = shift(jnp.concatenate([rap[5:], ram[5:]], axis=0), "gx", 1)
    fxm = shift(jnp.concatenate([rap[:5], ram[:5]], axis=0), "gx", -1)
    orbitals = B // pair_mask.shape[-1]
    limits = jnp.repeat(counts, orbitals, axis=-1).reshape(2, B).astype(F32)
    return solve(rap, ram, rbp, rbm, rxp, rxm, fxp, fxm, own, rhs_rows, limits)


def solution(mesh):
    return jax.shard_map(
        shards,
        mesh=mesh,
        in_specs=(
            P("gx", "gy", None, None, None),
            P("gx", "gy", None, None, None),
            P("gx", "gy", None, None, None),
            P("gx", "gy", None),
        ),
        out_specs=P("gx", "gy", None, None, None),
        check_vma=False,
    )
```

```python
import jax
import jax.numpy as jnp
from jax import lax
from jax.experimental import pallas as pl
from jax.experimental.pallas import tpu as pltpu
from jax.sharding import PartitionSpec as P

ITERS = 3
B = 128
POWERS = 2 * ITERS + 1
F32 = jnp.float32
BF16 = jnp.bfloat16
PREPARE_BYTES = 80 * 2**20


def off(u, v):
    return 3 * (u + 1) + (v + 1)


def edge_list(v):
    low, high = min(0, v), max(0, v)
    first = []
    for row, us in ((0, (-1, 0)), (1, (0, 1))):
        first += [(row, True, off(u, w)) for u in us for w in (low, high)]
        first.append((row, False, off(-1 if row == 0 else 1, v)))
    second = []
    for row, u in ((0, 1), (1, -1)):
        second += [(row, True, off(u, w)) for w in (low, high)]
        second += [(row, False, off(0, v)), (row, False, off(u, v))]
    return first, second


def own_list(u):
    row, us = (1, (0, 1)) if u > 0 else (0, (-1, 0))
    return [(row, True, off(w, v)) for w in us for v in (-1, 0, 1)] + [(row, False, off(u, 0))]


FIRST = {v: edge_list(v)[0] for v in (1, -1)}
SECOND = {v: edge_list(v)[1] for v in (1, -1)}
OWN = {u: own_list(u) for u in (1, -1)}


PACKED = (FIRST[1], FIRST[-1], SECOND[1], SECOND[-1], OWN[1], OWN[-1])
TOTAL_COPIES = sum(len(entries) for entries in PACKED)


def pack_kernel(mask, blocks, rhs, *refs):
    sends, own, held, masked, in_sems, out_sems, own_sem = refs[:6], refs[6], *refs[7:]
    block_copies = []
    for row in range(2):
        for part in range(3):
            offsets = pl.ds(3 * part, 3)
            block_copies.append(
                pltpu.make_async_copy(
                    blocks.at[row, 0, offsets], held.at[row, offsets], in_sems.at[3 * row + part]
                )
            )
            block_copies[-1].start()
    out_copies = []

    def send(source, ref, place):
        out_copies.append(pltpu.make_async_copy(source, ref.at[place], out_sems.at[len(out_copies)]))
        out_copies[-1].start()

    for ref, entries in zip(sends, PACKED):
        for place, (row, is_coupling, o) in enumerate(entries):
            if not is_coupling:
                send(rhs.at[row, 0, o], ref, place)
    atoms = mask.shape[0] // 16
    orbitals = B // (mask.shape[0] // 16)
    lane = lax.broadcasted_iota(jnp.int32, (mask.shape[0], 2 * atoms * B), 1)
    entry = lax.broadcasted_iota(jnp.int32, (mask.shape[0], 2 * atoms * B), 0)
    select = (entry == lane // orbitals).astype(F32).astype(BF16)
    wide = lax.dot_general(
        mask[...].astype(F32).astype(BF16),
        select,
        (((0,), (0,)), ((), ())),
        preferred_element_type=F32,
    )
    for row in range(2):
        for o in range(9):
            if o % 3 == 0:
                block_copies[3 * row + o // 3].wait()
            for a in range(atoms):
                start = (row * atoms + a) * B
                factor = jnp.broadcast_to(wide[o : o + 1, start : start + B], (orbitals, B))
                rows = slice(a * orbitals, (a + 1) * orbitals)
                masked[row, o, rows, :] = held[row, o, rows, :] * factor
            for ref, entries in zip(sends, PACKED):
                for place, listed in enumerate(entries):
                    if listed == (row, True, o):
                        send(masked.at[row, o], ref, place)
    own_copy = pltpu.make_async_copy(masked, own, own_sem)
    own_copy.start()
    for copy in out_copies:
        copy.wait()
    own_copy.wait()


def pack(blocks, mask, rhs):
    out = [jax.ShapeDtypeStruct((len(entries), B, B), F32) for entries in PACKED]
    out.append(jax.ShapeDtypeStruct((2, 9, B, B), F32))
    flat = jnp.transpose(mask, (0, 1, 3, 4, 2)).reshape(-1, 9)
    return pl.pallas_call(
        pack_kernel,
        out_shape=out,
        in_specs=[pl.BlockSpec(memory_space=pltpu.VMEM)] + [pl.BlockSpec(memory_space=pl.ANY)] * 2,
        out_specs=[pl.BlockSpec(memory_space=pl.ANY)] * 7,
        scratch_shapes=[
            pltpu.VMEM((2, 9, B, B), F32),
            pltpu.VMEM((2, 9, B, B), F32),
            pltpu.SemaphoreType.DMA((6,)),
            pltpu.SemaphoreType.DMA((TOTAL_COPIES,)),
            pltpu.SemaphoreType.DMA,
        ],
        compiler_params=pltpu.CompilerParams(vmem_limit_bytes=60 * 2**20),
        name="pack",
    )(flat, blocks, rhs)


def split(value):
    high = value.astype(BF16)
    low = (value - high.astype(F32)).astype(BF16)
    return high, low


def guarded(top, bottom, floor_val):
    return top * bottom / (bottom * bottom + floor_val * floor_val)


def poly_add(left, scale, right):
    out = []
    for i in range(max(len(left), len(right))):
        if i >= len(right):
            out.append(left[i])
        elif i >= len(left):
            out.append(scale * right[i])
        else:
            out.append(left[i] + scale * right[i])
    return out


def poly_apply(p):
    return poly_add(list(p), -1.0, [jnp.zeros_like(p[0])] + list(p))


def poly_first(gram, p):
    total = p[0] * gram[0][0]
    for i in range(1, len(p)):
        total = total + p[i] * gram[0][i]
    return total


def poly_norm(gram, p):
    total = 0.0
    for i in range(len(p)):
        inner = p[i] * gram[i][i]
        for j in range(i):
            inner = inner + 2.0 * (p[j] * gram[j][i])
        total = total + p[i] * inner
    return total


def tfqmr(gram, limits):
    one = jnp.ones_like(limits)
    zero = jnp.zeros_like(limits)
    norm = gram[0][0]
    w = [one]
    y1 = [one]
    u1 = poly_apply(y1)
    v = u1
    d = [zero]
    x = [zero]
    rho, floor_val, tau = norm, 0.1 * norm, jnp.sqrt(norm)
    theta = zero
    eta = zero
    y2 = None
    u2 = None
    ww = norm
    for iteration in range(ITERS):
        if iteration > 0:
            rho_next = poly_first(gram, w)
            beta = guarded(rho_next, rho, floor_val)
            floor_val = 0.1 * jnp.sqrt(norm * ww)
            rho = rho_next
            y1 = poly_add(w, beta, y2)
            u1 = poly_apply(y1)
            v = poly_add(u1, beta, poly_add(u2, beta, v))
        alpha_floor = 0.1 * jnp.sqrt(norm * (poly_norm(gram, v) + 1e-06))
        alpha = guarded(rho, poly_first(gram, v), alpha_floor)
        ratio = guarded(1.0, alpha, 0.1)
        y2 = poly_add(y1, -alpha, v)
        u2 = poly_apply(y2)
        active = (limits > iteration).astype(F32)
        for y, u in ((y1, u1), (y2, u2)):
            w = poly_add(w, -alpha, u)
            d = poly_add(y, theta * theta * eta * ratio, d)
            ww = poly_norm(gram, w)
            theta = jnp.sqrt(ww) / tau
            cosine = 1.0 / jnp.sqrt(1.0 + theta * theta)
            tau = tau * theta * cosine
            eta = cosine * cosine * alpha
            x = poly_add(x, active * eta, d)
    return x


COLUMNS = ((0, 2), (0, 3), (1, 3))
ROWS = ((0, 2), (0, 3), (1, 4), (2, 4))


def coupling_lanes(h, c, o):
    source_row, source_col = h + o // 3 - 1, c + o % 3 - 1
    c_low, c_high = COLUMNS[c]
    place = (source_row - ROWS[h][0]) * (c_high - c_low) + source_col - c_low
    return slice(place * B, (place + 1) * B)


def prepare_kernel(rap, ram, rbp, rbm, rxp, rxm, own, rhs, middle_h, middle_l, outer_h, outer_l, start):
    def put(h, c, is_coupling, o, value):
        if is_coupling:
            high, low = split(value)
            lanes = coupling_lanes(h, c, o)
            if h in (1, 2):
                middle_h[h - 1, c, :, lanes] = high
                middle_l[h - 1, c, :, lanes] = low
            else:
                outer_h[h // 3, :, lanes] = high
                outer_l[h // 3, :, lanes] = low
        else:
            g = h + o // 3 - 2
            if 0 <= g <= 1:
                start[g, 3 * (h - g) + c] = value

    for v, ref_a, ref_b in ((1, rap, rbp), (-1, ram, rbm)):
        for ref, entries in ((ref_a, FIRST[v]), (ref_b, SECOND[v])):
            for place, (row, is_coupling, o) in enumerate(entries):
                put(row + 1, 1 - v, is_coupling, o, ref[place])
    for u, ref in ((1, rxp), (-1, rxm)):
        for place, (row, is_coupling, o) in enumerate(OWN[u]):
            put(0 if u > 0 else 3, 1, is_coupling, o, ref[place])
    for row in range(2):
        for o in range(9):
            put(row + 1, 1, True, o, own[row, o])
    for row, u in ((0, 0), (1, 0), (0, 1), (1, -1)):
        put(row + 1, 1, False, off(u, 0), rhs[row, 0, off(u, 0)])


def prepare(*arrays):
    shapes = [((2, 3, B, 9 * B), BF16)] * 2 + [((2, B, 6 * B), BF16)] * 2 + [((2, 9, B, B), F32)]
    return pl.pallas_call(
        prepare_kernel,
        out_shape=[jax.ShapeDtypeStruct(*shape) for shape in shapes],
        in_specs=[pl.BlockSpec(memory_space=pltpu.VMEM)] * len(arrays),
        out_specs=[pl.BlockSpec(memory_space=pltpu.VMEM)] * len(shapes),
        compiler_params=pltpu.CompilerParams(vmem_limit_bytes=16 * 2**20),
        cost_estimate=pl.CostEstimate(flops=0, bytes_accessed=PREPARE_BYTES, transcendentals=0),
        name="prepare",
    )(*arrays)


def solve_kernel(
    middle_h, middle_l, outer_h, outer_l, start, fpl, fpr, fml, fmr, limits, out, corner_h, corner_l, *scratch
):
    fields = (scratch[0:3], scratch[3:6])
    later = scratch[6:]
    corners = {}
    for u, refs in ((1, (fpl, fpr)), (-1, (fml, fmr))):
        part = 5 if u > 0 else 0
        for side, v in ((0, 1), (1, -1)):
            for place in range(5):
                corners[0 if u > 0 else 3, 1 - v, *FIRST[v][part + place][1:]] = (refs[side], place)

    def power(slot, g, m):
        if slot > 0:
            return later[slot - 1][g, m * B : (m + 1) * B, :]
        h, c = g + m // 3, m % 3
        found = corners.get((h, c, False, off(1 - m // 3, 1 - c)))
        if found is not None and h in (0, 3):
            return found[0][found[1]]
        return start[g, m]

    def put_field(slot, g, h, c, value):
        high, low = split(value)
        for target in range(3):
            c_low, c_high = COLUMNS[target]
            if c_low <= c < c_high:
                first = (h * (c_high - c_low) + c - c_low) * B
                ref = fields[slot % 2][target]
                ref[first : first + B, (1 + g) * B : (2 + g) * B] = high
                ref[first : first + B, 3 * g * B : (3 * g + 1) * B] = low

    def put_vector(slot, g, h, c, value):
        m = 3 * (h - g) + c
        later[slot - 1][g, m * B : (m + 1) * B, :] = value
        if slot < POWERS - 1:
            put_field(slot, g, h, c, value)

    for (h, c, is_coupling, o), (ref, place) in corners.items():
        if is_coupling:
            high, low = split(ref[place])
            corner_h[h // 3, c // 2, :, coupling_lanes(h, c, o)] = high
            corner_l[h // 3, c // 2, :, coupling_lanes(h, c, o)] = low
    for g in range(2):
        for m in range(9):
            put_field(0, g, g + m // 3, m % 3, power(0, g, m))

    def weights(h, c):
        if h in (1, 2):
            return middle_h.at[h - 1, c], middle_l.at[h - 1, c]
        if c == 1:
            return outer_h.at[h // 3], outer_l.at[h // 3]
        return corner_h.at[h // 3, c // 2], corner_l.at[h // 3, c // 2]

    def apply(slot):
        for h in range(4):
            for c in range(3):
                field = fields[slot % 2][c]
                count = COLUMNS[c][1] - COLUMNS[c][0]
                first = ROWS[h][0]
                wh, wl = weights(h, c)

                def product(weight, low, high, lanes_low, lanes_high):
                    left = weight[:, (low - first) * count * B : (high - first) * count * B]
                    right = field[low * count * B : high * count * B, lanes_low * B : lanes_high * B]
                    return jnp.dot(left, right, preferred_element_type=F32)

                values = {}
                for g in range(2):
                    if 0 <= h - g <= 2:
                        low, high = max(ROWS[h][0], g), min(ROWS[h][1], g + 3)
                        both = product(wh, low, high, 2 * g, 2 * g + 2)
                        values[g] = both[:, :B] + both[:, B:]
                if len(values) == 2:
                    both = product(wl, 1, 3, 1, 3)
                    values[0] = values[0] + both[:, :B]
                    values[1] = values[1] + both[:, B:]
                    g, other = (0, 0) if h == 1 else (1, 3)
                    values[g] = values[g] + product(wl, other, other + 1, 1 + g, 2 + g)
                else:
                    for g in values:
                        values[g] = values[g] + product(wl, *ROWS[h], 1 + g, 2 + g)
                for g in values:
                    put_vector(slot + 1, g, h, c, values[g])

    partial = {}

    def grams(slot):
        for g in range(2):
            totals = [None] * (slot + 1)
            for m in range(9):
                here = power(slot, g, m)
                for i in range(slot + 1):
                    term = jnp.sum((here * power(i, g, m)).reshape(16, 8, B), axis=0)
                    totals[i] = term if totals[i] is None else totals[i] + term
            for i in range(slot + 1):
                partial[slot, i, g] = jnp.sum(totals[i], axis=0, keepdims=True)

    for slot in range(POWERS - 1):
        apply(slot)
        grams(slot)
    grams(POWERS - 1)
    gram = [
        [
            jnp.concatenate([partial[max(i, j), min(i, j), g] for g in range(2)], axis=0)
            for j in range(POWERS)
        ]
        for i in range(POWERS)
    ]
    x = tfqmr(gram, limits[...])
    for g in range(2):
        for m in range(9):
            total = x[0][g : g + 1, :] * power(0, g, m)
            for i in range(1, len(x)):
                total = total + x[i][g : g + 1, :] * power(i, g, m)
            out[g, 0, m] = total


def solve(*arrays):
    fields = [pltpu.VMEM((4 * (high - low) * B, 4 * B), BF16) for low, high in COLUMNS]
    return pl.pallas_call(
        solve_kernel,
        out_shape=jax.ShapeDtypeStruct((2, 1, 9, B, B), F32),
        in_specs=[pl.BlockSpec(memory_space=pltpu.VMEM)] * len(arrays),
        out_specs=pl.BlockSpec(memory_space=pltpu.VMEM),
        scratch_shapes=[
            pltpu.VMEM((2, 2, B, 4 * B), BF16),
            pltpu.VMEM((2, 2, B, 4 * B), BF16),
            *fields,
            *fields,
            *[pltpu.VMEM((2, 9 * B, B), F32) for _ in range(POWERS - 1)],
        ],
        compiler_params=pltpu.CompilerParams(vmem_limit_bytes=24 * 2**20),
        name="solve",
    )(*arrays)


def shift(value, axis, step):
    count = lax.axis_size(axis)
    if step > 0:
        pairs = [(i, i + 1) for i in range(count - 1)]
    else:
        pairs = [(i + 1, i) for i in range(count - 1)]
    return lax.ppermute(value, axis, pairs)


def shards(blocks, pair_mask, rhs_rows, counts):
    sap, sam, sbp, sbm, oxp, oxm, own = pack(blocks, pair_mask, rhs_rows)
    rap = shift(sap, "gy", 1)
    ram = shift(sam, "gy", -1)
    rxp = shift(oxp, "gx", 1)
    rxm = shift(oxm, "gx", -1)
    rbp = shift(sbp, "gy", 1)
    rbm = shift(sbm, "gy", -1)
    fxp = (shift(rap[5:], "gx", 1), shift(ram[5:], "gx", 1))
    fxm = (shift(rap[:5], "gx", -1), shift(ram[:5], "gx", -1))
    prepared = prepare(rap, ram, rbp, rbm, rxp, rxm, own, rhs_rows)
    orbitals = B // pair_mask.shape[-1]
    limits = jnp.repeat(counts, orbitals, axis=-1).reshape(2, B).astype(F32)
    return solve(*prepared, *fxp, *fxm, limits)


def solution(mesh):
    return jax.shard_map(
        shards,
        mesh=mesh,
        in_specs=(
            P("gx", "gy", None, None, None),
            P("gx", "gy", None, None, None),
            P("gx", "gy", None, None, None),
            P("gx", "gy", None),
        ),
        out_specs=P("gx", "gy", None, None, None),
        check_vma=False,
    )
```

```python
import jax
import jax.numpy as jnp
from jax import lax
from jax.experimental import pallas as pl
from jax.experimental.pallas import tpu as pltpu
from jax.sharding import PartitionSpec as P

ITERS = 3
B = 128
POWERS = 2 * ITERS + 1
F32 = jnp.float32
BF16 = jnp.bfloat16


def off(u, v):
    return 3 * (u + 1) + (v + 1)


def edge_list(v):
    low, high = min(0, v), max(0, v)
    first = []
    for row, us in ((0, (-1, 0)), (1, (0, 1))):
        first += [(row, True, off(u, w)) for u in us for w in (low, high)]
        first.append((row, False, off(-1 if row == 0 else 1, v)))
    second = []
    for row, u in ((0, 1), (1, -1)):
        second += [(row, True, off(u, w)) for w in (low, high)]
        second += [(row, False, off(0, v)), (row, False, off(u, v))]
    return first, second


def own_list(u):
    row, us = (1, (0, 1)) if u > 0 else (0, (-1, 0))
    return [(row, True, off(w, v)) for w in us for v in (-1, 0, 1)] + [(row, False, off(u, 0))]


FIRST = {v: edge_list(v)[0] for v in (1, -1)}
SECOND = {v: edge_list(v)[1] for v in (1, -1)}
OWN = {u: own_list(u) for u in (1, -1)}


PACKED = (FIRST[1], FIRST[-1], SECOND[1], SECOND[-1], OWN[1], OWN[-1])


def masked_blocks(mask, blocks):
    atoms = mask.shape[0] // 16
    orbitals = B // atoms
    lane = lax.broadcasted_iota(jnp.int32, (mask.shape[0], 2 * atoms * B), 1)
    entry = lax.broadcasted_iota(jnp.int32, (mask.shape[0], 2 * atoms * B), 0)
    select = (entry == lane // orbitals).astype(F32).astype(BF16)
    wide = lax.dot_general(
        mask[...].astype(F32).astype(BF16),
        select,
        (((0,), (0,)), ((), ())),
        preferred_element_type=F32,
    )
    for row in range(2):
        for o in range(9):
            rows = []
            for a in range(atoms):
                start = (row * atoms + a) * B
                rows.append(jnp.broadcast_to(wide[o : o + 1, start : start + B], (orbitals, B)))
            yield row, o, blocks[row, 0, o] * jnp.concatenate(rows, axis=0)


def pack_kernel(mask, blocks, rhs, *sends):
    for row, o, value in masked_blocks(mask, blocks):
        for ref, entries in zip(sends, PACKED):
            for place, listed in enumerate(entries):
                if listed == (row, True, o):
                    ref[place] = value
    for ref, entries in zip(sends, PACKED):
        for place, (row, is_coupling, o) in enumerate(entries):
            if not is_coupling:
                ref[place] = rhs[row, 0, o]


def pack(blocks, mask, rhs):
    out = [jax.ShapeDtypeStruct((len(entries), B, B), F32) for entries in PACKED]
    return pl.pallas_call(
        pack_kernel,
        out_shape=out,
        in_specs=[pl.BlockSpec(memory_space=pltpu.VMEM)] + [pl.BlockSpec(memory_space=pltpu.VMEM)] * 2,
        out_specs=[pl.BlockSpec(memory_space=pltpu.VMEM)] * 6,
        compiler_params=pltpu.CompilerParams(vmem_limit_bytes=8 * 2**20),
        name="pack",
    )(mask, blocks, rhs)


def relay_kernel(rap, ram, up, down):
    up[:5] = rap[5:]
    up[5:] = ram[5:]
    down[:5] = rap[:5]
    down[5:] = ram[:5]


def relay(rap, ram):
    return pl.pallas_call(
        relay_kernel,
        out_shape=[jax.ShapeDtypeStruct((10, B, B), F32)] * 2,
        in_specs=[pl.BlockSpec(memory_space=pltpu.VMEM)] * 2,
        out_specs=[pl.BlockSpec(memory_space=pltpu.VMEM)] * 2,
        compiler_params=pltpu.CompilerParams(vmem_limit_bytes=8 * 2**20),
        name="relay",
    )(rap, ram)


def split(value):
    high = value.astype(BF16)
    low = (value - high.astype(F32)).astype(BF16)
    return high, low


def guarded(top, bottom, floor_val):
    return top * bottom / (bottom * bottom + floor_val * floor_val)


def poly_add(left, scale, right):
    out = []
    for i in range(max(len(left), len(right))):
        if i >= len(right):
            out.append(left[i])
        elif i >= len(left):
            out.append(scale * right[i])
        else:
            out.append(left[i] + scale * right[i])
    return out


def poly_apply(p):
    return poly_add(list(p), -1.0, [jnp.zeros_like(p[0])] + list(p))


def poly_first(gram, p):
    total = p[0] * gram[0][0]
    for i in range(1, len(p)):
        total = total + p[i] * gram[0][i]
    return total


def poly_norm(gram, p):
    total = 0.0
    for i in range(len(p)):
        inner = p[i] * gram[i][i]
        for j in range(i):
            inner = inner + 2.0 * (p[j] * gram[j][i])
        total = total + p[i] * inner
    return total


def tfqmr(gram, limits):
    one = jnp.ones_like(limits)
    zero = jnp.zeros_like(limits)
    norm = gram[0][0]
    w = [one]
    y1 = [one]
    u1 = poly_apply(y1)
    v = u1
    d = [zero]
    x = [zero]
    rho, floor_val, tau = norm, 0.1 * norm, jnp.sqrt(norm)
    theta = zero
    eta = zero
    y2 = None
    u2 = None
    ww = norm
    for iteration in range(ITERS):
        if iteration > 0:
            rho_next = poly_first(gram, w)
            beta = guarded(rho_next, rho, floor_val)
            floor_val = 0.1 * jnp.sqrt(norm * ww)
            rho = rho_next
            y1 = poly_add(w, beta, y2)
            u1 = poly_apply(y1)
            v = poly_add(u1, beta, poly_add(u2, beta, v))
        alpha_floor = 0.1 * jnp.sqrt(norm * (poly_norm(gram, v) + 1e-06))
        alpha = guarded(rho, poly_first(gram, v), alpha_floor)
        ratio = guarded(1.0, alpha, 0.1)
        y2 = poly_add(y1, -alpha, v)
        u2 = poly_apply(y2)
        active = (limits > iteration).astype(F32)
        for y, u in ((y1, u1), (y2, u2)):
            w = poly_add(w, -alpha, u)
            d = poly_add(y, theta * theta * eta * ratio, d)
            ww = poly_norm(gram, w)
            theta = jnp.sqrt(ww) / tau
            cosine = 1.0 / jnp.sqrt(1.0 + theta * theta)
            tau = tau * theta * cosine
            eta = cosine * cosine * alpha
            x = poly_add(x, active * eta, d)
    return x


COLUMNS = ((0, 2), (0, 3), (1, 3))
ROWS = ((0, 2), (0, 3), (1, 4), (2, 4))


def coupling_lanes(h, c, o):
    source_row, source_col = h + o // 3 - 1, c + o % 3 - 1
    c_low, c_high = COLUMNS[c]
    place = (source_row - ROWS[h][0]) * (c_high - c_low) + source_col - c_low
    return slice(place * B, (place + 1) * B)


def prepare_kernel(rap, ram, rbp, rbm, rxp, rxm, mask, blocks, rhs, middle_h, middle_l, outer_h, outer_l, start):
    def put(h, c, is_coupling, o, value):
        if is_coupling:
            high, low = split(value)
            lanes = coupling_lanes(h, c, o)
            if h in (1, 2):
                middle_h[h - 1, c, :, lanes] = high
                middle_l[h - 1, c, :, lanes] = low
            else:
                outer_h[h // 3, :, lanes] = high
                outer_l[h // 3, :, lanes] = low
        else:
            g = h + o // 3 - 2
            if 0 <= g <= 1:
                start[g, 3 * (h - g) + c] = value

    for v, ref_a, ref_b in ((1, rap, rbp), (-1, ram, rbm)):
        for ref, entries in ((ref_a, FIRST[v]), (ref_b, SECOND[v])):
            for place, (row, is_coupling, o) in enumerate(entries):
                put(row + 1, 1 - v, is_coupling, o, ref[place])
    for u, ref in ((1, rxp), (-1, rxm)):
        for place, (row, is_coupling, o) in enumerate(OWN[u]):
            put(0 if u > 0 else 3, 1, is_coupling, o, ref[place])
    for row, o, value in masked_blocks(mask, blocks):
        put(row + 1, 1, True, o, value)
    for row, u in ((0, 0), (1, 0), (0, 1), (1, -1)):
        put(row + 1, 1, False, off(u, 0), rhs[row, 0, off(u, 0)])


def prepare(*arrays):
    shapes = [((2, 3, B, 9 * B), BF16)] * 2 + [((2, B, 6 * B), BF16)] * 2 + [((2, 9, B, B), F32)]
    return pl.pallas_call(
        prepare_kernel,
        out_shape=[jax.ShapeDtypeStruct(*shape) for shape in shapes],
        in_specs=[pl.BlockSpec(memory_space=pltpu.VMEM)] * len(arrays),
        out_specs=[pl.BlockSpec(memory_space=pltpu.VMEM)] * len(shapes),
        compiler_params=pltpu.CompilerParams(vmem_limit_bytes=16 * 2**20),
        cost_estimate=pl.CostEstimate(flops=10**12, bytes_accessed=10**9, transcendentals=10**9),
        name="prepare",
    )(*arrays)


def solve_kernel(
    middle_h, middle_l, outer_h, outer_l, start, fxp, fxm, limits, out, corner_h, corner_l, *scratch
):
    fields = (scratch[0:3], scratch[3:6])
    later = scratch[6:]
    corners = {}
    for u, ref in ((1, fxp), (-1, fxm)):
        part = 5 if u > 0 else 0
        for side, v in ((0, 1), (1, -1)):
            for place in range(5):
                corners[0 if u > 0 else 3, 1 - v, *FIRST[v][part + place][1:]] = (ref, side * 5 + place)

    def power(slot, g, m):
        if slot > 0:
            return later[slot - 1][g, m * B : (m + 1) * B, :]
        h, c = g + m // 3, m % 3
        found = corners.get((h, c, False, off(1 - m // 3, 1 - c)))
        if found is not None and h in (0, 3):
            return found[0][found[1]]
        return start[g, m]

    def put_field(slot, g, h, c, value):
        high, low = split(value)
        for target in range(3):
            c_low, c_high = COLUMNS[target]
            if c_low <= c < c_high:
                first = (h * (c_high - c_low) + c - c_low) * B
                ref = fields[slot % 2][target]
                ref[first : first + B, (1 + g) * B : (2 + g) * B] = high
                ref[first : first + B, 3 * g * B : (3 * g + 1) * B] = low

    def put_vector(slot, g, h, c, value):
        m = 3 * (h - g) + c
        later[slot - 1][g, m * B : (m + 1) * B, :] = value
        if slot < POWERS - 1:
            put_field(slot, g, h, c, value)

    for (h, c, is_coupling, o), (ref, place) in corners.items():
        if is_coupling:
            high, low = split(ref[place])
            corner_h[h // 3, c // 2, :, coupling_lanes(h, c, o)] = high
            corner_l[h // 3, c // 2, :, coupling_lanes(h, c, o)] = low
    for g in range(2):
        for m in range(9):
            put_field(0, g, g + m // 3, m % 3, power(0, g, m))

    def weights(h, c):
        if h in (1, 2):
            return middle_h.at[h - 1, c], middle_l.at[h - 1, c]
        if c == 1:
            return outer_h.at[h // 3], outer_l.at[h // 3]
        return corner_h.at[h // 3, c // 2], corner_l.at[h // 3, c // 2]

    def apply(slot):
        for h in range(4):
            for c in range(3):
                field = fields[slot % 2][c]
                count = COLUMNS[c][1] - COLUMNS[c][0]
                first = ROWS[h][0]
                wh, wl = weights(h, c)

                def product(weight, low, high, lanes_low, lanes_high):
                    left = weight[:, (low - first) * count * B : (high - first) * count * B]
                    right = field[low * count * B : high * count * B, lanes_low * B : lanes_high * B]
                    return jnp.dot(left, right, preferred_element_type=F32)

                values = {}
                for g in range(2):
                    if 0 <= h - g <= 2:
                        low, high = max(ROWS[h][0], g), min(ROWS[h][1], g + 3)
                        both = product(wh, low, high, 2 * g, 2 * g + 2)
                        values[g] = both[:, :B] + both[:, B:]
                if len(values) == 2:
                    both = product(wl, 1, 3, 1, 3)
                    values[0] = values[0] + both[:, :B]
                    values[1] = values[1] + both[:, B:]
                    g, other = (0, 0) if h == 1 else (1, 3)
                    values[g] = values[g] + product(wl, other, other + 1, 1 + g, 2 + g)
                else:
                    for g in values:
                        values[g] = values[g] + product(wl, *ROWS[h], 1 + g, 2 + g)
                for g in values:
                    put_vector(slot + 1, g, h, c, values[g])

    partial = {}

    def grams(slot):
        for g in range(2):
            totals = [None] * (slot + 1)
            for m in range(9):
                here = power(slot, g, m)
                for i in range(slot + 1):
                    term = jnp.sum((here * power(i, g, m)).reshape(16, 8, B), axis=0)
                    totals[i] = term if totals[i] is None else totals[i] + term
            for i in range(slot + 1):
                partial[slot, i, g] = jnp.sum(totals[i], axis=0, keepdims=True)

    for slot in range(POWERS - 1):
        apply(slot)
        grams(slot)
    grams(POWERS - 1)
    gram = [
        [
            jnp.concatenate([partial[max(i, j), min(i, j), g] for g in range(2)], axis=0)
            for j in range(POWERS)
        ]
        for i in range(POWERS)
    ]
    x = tfqmr(gram, limits[...])
    for g in range(2):
        for m in range(9):
            total = x[0][g : g + 1, :] * power(0, g, m)
            for i in range(1, len(x)):
                total = total + x[i][g : g + 1, :] * power(i, g, m)
            out[g, 0, m] = total


def solve(*arrays):
    fields = [pltpu.VMEM((4 * (high - low) * B, 4 * B), BF16) for low, high in COLUMNS]
    return pl.pallas_call(
        solve_kernel,
        out_shape=jax.ShapeDtypeStruct((2, 1, 9, B, B), F32),
        in_specs=[pl.BlockSpec(memory_space=pltpu.VMEM)] * len(arrays),
        out_specs=pl.BlockSpec(memory_space=pltpu.VMEM),
        scratch_shapes=[
            pltpu.VMEM((2, 2, B, 4 * B), BF16),
            pltpu.VMEM((2, 2, B, 4 * B), BF16),
            *fields,
            *fields,
            *[pltpu.VMEM((2, 9 * B, B), F32) for _ in range(POWERS - 1)],
        ],
        compiler_params=pltpu.CompilerParams(vmem_limit_bytes=24 * 2**20),
        name="solve",
    )(*arrays)


def shift(value, axis, step):
    count = lax.axis_size(axis)
    if step > 0:
        pairs = [(i, i + 1) for i in range(count - 1)]
    else:
        pairs = [(i + 1, i) for i in range(count - 1)]
    return lax.ppermute(value, axis, pairs)


def shards(blocks, pair_mask, rhs_rows, counts):
    mask = jnp.transpose(pair_mask, (0, 1, 3, 4, 2)).reshape(-1, 9)
    sap, sam, sbp, sbm, oxp, oxm = pack(blocks, mask, rhs_rows)
    rap = shift(sap, "gy", 1)
    ram = shift(sam, "gy", -1)
    rxp = shift(oxp, "gx", 1)
    rxm = shift(oxm, "gx", -1)
    rbp = shift(sbp, "gy", 1)
    rbm = shift(sbm, "gy", -1)
    up, down = relay(rap, ram)
    fxp = shift(up, "gx", 1)
    fxm = shift(down, "gx", -1)
    prepared = prepare(rap, ram, rbp, rbm, rxp, rxm, mask, blocks, rhs_rows)
    orbitals = B // pair_mask.shape[-1]
    limits = jnp.repeat(counts, orbitals, axis=-1).reshape(2, B).astype(F32)
    return solve(*prepared, fxp, fxm, limits)


def solution(mesh):
    return jax.shard_map(
        shards,
        mesh=mesh,
        in_specs=(
            P("gx", "gy", None, None, None),
            P("gx", "gy", None, None, None),
            P("gx", "gy", None, None, None),
            P("gx", "gy", None),
        ),
        out_specs=P("gx", "gy", None, None, None),
        check_vma=False,
    )
```

```python
import jax
import jax.numpy as jnp
from jax import lax
from jax.experimental import pallas as pl
from jax.experimental.pallas import tpu as pltpu
from jax.sharding import PartitionSpec as P

ITERS = 3
B = 128
POWERS = 2 * ITERS + 1
F32 = jnp.float32
BF16 = jnp.bfloat16


def off(u, v):
    return 3 * (u + 1) + (v + 1)


def edge_list(v):
    low, high = min(0, v), max(0, v)
    first = []
    for row, us in ((0, (-1, 0)), (1, (0, 1))):
        first += [(row, True, off(u, w)) for u in us for w in (low, high)]
        first.append((row, False, off(-1 if row == 0 else 1, v)))
    second = []
    for row, u in ((0, 1), (1, -1)):
        second += [(row, True, off(u, w)) for w in (low, high)]
        second += [(row, False, off(0, v)), (row, False, off(u, v))]
    return first, second


def own_list(u):
    row, us = (1, (0, 1)) if u > 0 else (0, (-1, 0))
    return [(row, True, off(w, v)) for w in us for v in (-1, 0, 1)] + [(row, False, off(u, 0))]


FIRST = {v: edge_list(v)[0] for v in (1, -1)}
SECOND = {v: edge_list(v)[1] for v in (1, -1)}
OWN = {u: own_list(u) for u in (1, -1)}


PACKED = (FIRST[1], FIRST[-1], SECOND[1], SECOND[-1])


def masked_blocks(mask, blocks):
    atoms = mask.shape[0] // 16
    orbitals = B // atoms
    lane = lax.broadcasted_iota(jnp.int32, (mask.shape[0], 2 * atoms * B), 1)
    entry = lax.broadcasted_iota(jnp.int32, (mask.shape[0], 2 * atoms * B), 0)
    select = (entry == lane // orbitals).astype(F32).astype(BF16)
    wide = lax.dot_general(
        mask[...].astype(F32).astype(BF16),
        select,
        (((0,), (0,)), ((), ())),
        preferred_element_type=F32,
    )
    for row in range(2):
        for o in range(9):
            rows = []
            for a in range(atoms):
                start = (row * atoms + a) * B
                rows.append(jnp.broadcast_to(wide[o : o + 1, start : start + B], (orbitals, B)))
            yield row, o, blocks[row, 0, o] * jnp.concatenate(rows, axis=0)


def place_blocks(mask, blocks, rhs, targets):
    for row, o, value in masked_blocks(mask, blocks):
        for ref, entries in targets:
            for place, listed in enumerate(entries):
                if listed == (row, True, o):
                    ref[place] = value
    for ref, entries in targets:
        for place, (row, is_coupling, o) in enumerate(entries):
            if not is_coupling:
                ref[place] = rhs[row, 0, o]


def pack_kernel(mask, blocks, rhs, *sends):
    place_blocks(mask, blocks, rhs, list(zip(sends, PACKED)))


def pack(blocks, mask, rhs):
    out = [jax.ShapeDtypeStruct((len(entries), B, B), F32) for entries in PACKED]
    return pl.pallas_call(
        pack_kernel,
        out_shape=out,
        in_specs=[pl.BlockSpec(memory_space=pltpu.VMEM)] + [pl.BlockSpec(memory_space=pltpu.VMEM)] * 2,
        out_specs=[pl.BlockSpec(memory_space=pltpu.VMEM)] * 4,
        compiler_params=pltpu.CompilerParams(vmem_limit_bytes=8 * 2**20),
        name="pack",
    )(mask, blocks, rhs)


def relay_kernel(mask, blocks, rhs, rap, ram, up, down):
    place_blocks(mask, blocks, rhs, [(up, OWN[1]), (down, OWN[-1])])
    up[7:12] = rap[5:]
    up[12:] = ram[5:]
    down[7:12] = rap[:5]
    down[12:] = ram[:5]


def relay(*arrays):
    return pl.pallas_call(
        relay_kernel,
        out_shape=[jax.ShapeDtypeStruct((17, B, B), F32)] * 2,
        in_specs=[pl.BlockSpec(memory_space=pltpu.VMEM)] * 5,
        out_specs=[pl.BlockSpec(memory_space=pltpu.VMEM)] * 2,
        compiler_params=pltpu.CompilerParams(vmem_limit_bytes=8 * 2**20),
        name="relay",
    )(*arrays)


def split(value):
    high = value.astype(BF16)
    low = (value - high.astype(F32)).astype(BF16)
    return high, low


def guarded(top, bottom, floor_val):
    return top * bottom / (bottom * bottom + floor_val * floor_val)


def poly_add(left, scale, right):
    out = []
    for i in range(max(len(left), len(right))):
        if i >= len(right):
            out.append(left[i])
        elif i >= len(left):
            out.append(scale * right[i])
        else:
            out.append(left[i] + scale * right[i])
    return out


def poly_apply(p):
    return poly_add(list(p), -1.0, [jnp.zeros_like(p[0])] + list(p))


def poly_first(gram, p):
    total = p[0] * gram[0][0]
    for i in range(1, len(p)):
        total = total + p[i] * gram[0][i]
    return total


def poly_norm(gram, p):
    total = 0.0
    for i in range(len(p)):
        inner = p[i] * gram[i][i]
        for j in range(i):
            inner = inner + 2.0 * (p[j] * gram[j][i])
        total = total + p[i] * inner
    return total


def tfqmr(gram, limits):
    one = jnp.ones_like(limits)
    zero = jnp.zeros_like(limits)
    norm = gram[0][0]
    w = [one]
    y1 = [one]
    u1 = poly_apply(y1)
    v = u1
    d = [zero]
    x = [zero]
    rho, floor_val, tau = norm, 0.1 * norm, jnp.sqrt(norm)
    theta = zero
    eta = zero
    y2 = None
    u2 = None
    ww = norm
    for iteration in range(ITERS):
        if iteration > 0:
            rho_next = poly_first(gram, w)
            beta = guarded(rho_next, rho, floor_val)
            floor_val = 0.1 * jnp.sqrt(norm * ww)
            rho = rho_next
            y1 = poly_add(w, beta, y2)
            u1 = poly_apply(y1)
            v = poly_add(u1, beta, poly_add(u2, beta, v))
        alpha_floor = 0.1 * jnp.sqrt(norm * (poly_norm(gram, v) + 1e-06))
        alpha = guarded(rho, poly_first(gram, v), alpha_floor)
        ratio = guarded(1.0, alpha, 0.1)
        y2 = poly_add(y1, -alpha, v)
        u2 = poly_apply(y2)
        active = (limits > iteration).astype(F32)
        for y, u in ((y1, u1), (y2, u2)):
            w = poly_add(w, -alpha, u)
            d = poly_add(y, theta * theta * eta * ratio, d)
            ww = poly_norm(gram, w)
            theta = jnp.sqrt(ww) / tau
            cosine = 1.0 / jnp.sqrt(1.0 + theta * theta)
            tau = tau * theta * cosine
            eta = cosine * cosine * alpha
            x = poly_add(x, active * eta, d)
    return x


COLUMNS = ((0, 2), (0, 3), (1, 3))
ROWS = ((0, 2), (0, 3), (1, 4), (2, 4))


def coupling_lanes(h, c, o):
    source_row, source_col = h + o // 3 - 1, c + o % 3 - 1
    c_low, c_high = COLUMNS[c]
    place = (source_row - ROWS[h][0]) * (c_high - c_low) + source_col - c_low
    return slice(place * B, (place + 1) * B)


def prepare_kernel(rap, ram, rbp, rbm, mask, blocks, rhs, middle_h, middle_l, start):
    def put(h, c, is_coupling, o, value):
        if is_coupling:
            high, low = split(value)
            lanes = coupling_lanes(h, c, o)
            middle_h[h - 1, c, :, lanes] = high
            middle_l[h - 1, c, :, lanes] = low
        else:
            g = h + o // 3 - 2
            if 0 <= g <= 1:
                start[g, 3 * (h - g) + c] = value

    for v, ref_a, ref_b in ((1, rap, rbp), (-1, ram, rbm)):
        for ref, entries in ((ref_a, FIRST[v]), (ref_b, SECOND[v])):
            for place, (row, is_coupling, o) in enumerate(entries):
                put(row + 1, 1 - v, is_coupling, o, ref[place])
    for row, o, value in masked_blocks(mask, blocks):
        put(row + 1, 1, True, o, value)
    for row, u in ((0, 0), (1, 0), (0, 1), (1, -1)):
        put(row + 1, 1, False, off(u, 0), rhs[row, 0, off(u, 0)])


def prepare(*arrays):
    shapes = [((2, 3, B, 9 * B), BF16)] * 2 + [((2, 9, B, B), F32)]
    return pl.pallas_call(
        prepare_kernel,
        out_shape=[jax.ShapeDtypeStruct(*shape) for shape in shapes],
        in_specs=[pl.BlockSpec(memory_space=pltpu.VMEM)] * len(arrays),
        out_specs=[pl.BlockSpec(memory_space=pltpu.VMEM)] * len(shapes),
        compiler_params=pltpu.CompilerParams(vmem_limit_bytes=12 * 2**20),
        cost_estimate=pl.CostEstimate(flops=10**12, bytes_accessed=10**9, transcendentals=10**9),
        name="prepare",
    )(*arrays)


def solve_kernel(
    middle_h, middle_l, start, fxp, fxm, limits, out, outer_h, outer_l, *scratch
):
    fields = (scratch[0:3], scratch[3:6])
    later = scratch[6:]
    outer = {}
    for u, ref in ((1, fxp), (-1, fxm)):
        h = 0 if u > 0 else 3
        for place, (row, is_coupling, o) in enumerate(OWN[u]):
            outer[h, 1, is_coupling, o] = (ref, place)
        part = 5 if u > 0 else 0
        for side, v in ((0, 1), (1, -1)):
            for place in range(5):
                outer[h, 1 - v, *FIRST[v][part + place][1:]] = (ref, 7 + side * 5 + place)

    def power(slot, g, m):
        if slot > 0:
            return later[slot - 1][g, m * B : (m + 1) * B, :]
        h, c = g + m // 3, m % 3
        found = outer.get((h, c, False, off(1 - m // 3, 1 - c)))
        if found is not None:
            return found[0][found[1]]
        return start[g, m]

    def put_field(slot, g, h, c, value):
        high, low = split(value)
        for target in range(3):
            c_low, c_high = COLUMNS[target]
            if c_low <= c < c_high:
                first = (h * (c_high - c_low) + c - c_low) * B
                ref = fields[slot % 2][target]
                ref[first : first + B, (1 + g) * B : (2 + g) * B] = high
                ref[first : first + B, 3 * g * B : (3 * g + 1) * B] = low

    def put_vector(slot, g, h, c, value):
        m = 3 * (h - g) + c
        later[slot - 1][g, m * B : (m + 1) * B, :] = value
        if slot < POWERS - 1:
            put_field(slot, g, h, c, value)

    for (h, c, is_coupling, o), (ref, place) in outer.items():
        if is_coupling:
            high, low = split(ref[place])
            outer_h[h // 3, c, :, coupling_lanes(h, c, o)] = high
            outer_l[h // 3, c, :, coupling_lanes(h, c, o)] = low
    for g in range(2):
        for m in range(9):
            put_field(0, g, g + m // 3, m % 3, power(0, g, m))

    def weights(h, c):
        if h in (1, 2):
            return middle_h.at[h - 1, c], middle_l.at[h - 1, c]
        return outer_h.at[h // 3, c], outer_l.at[h // 3, c]

    def apply(slot):
        for h in range(4):
            for c in range(3):
                field = fields[slot % 2][c]
                count = COLUMNS[c][1] - COLUMNS[c][0]
                first = ROWS[h][0]
                wh, wl = weights(h, c)

                def product(weight, low, high, lanes_low, lanes_high):
                    left = weight[:, (low - first) * count * B : (high - first) * count * B]
                    right = field[low * count * B : high * count * B, lanes_low * B : lanes_high * B]
                    return jnp.dot(left, right, preferred_element_type=F32)

                values = {}
                for g in range(2):
                    if 0 <= h - g <= 2:
                        low, high = max(ROWS[h][0], g), min(ROWS[h][1], g + 3)
                        both = product(wh, low, high, 2 * g, 2 * g + 2)
                        values[g] = both[:, :B] + both[:, B:]
                if len(values) == 2:
                    both = product(wl, 1, 3, 1, 3)
                    values[0] = values[0] + both[:, :B]
                    values[1] = values[1] + both[:, B:]
                    g, other = (0, 0) if h == 1 else (1, 3)
                    values[g] = values[g] + product(wl, other, other + 1, 1 + g, 2 + g)
                else:
                    for g in values:
                        values[g] = values[g] + product(wl, *ROWS[h], 1 + g, 2 + g)
                for g in values:
                    put_vector(slot + 1, g, h, c, values[g])

    partial = {}

    def grams(slot):
        for g in range(2):
            totals = [None] * (slot + 1)
            for m in range(9):
                here = power(slot, g, m)
                for i in range(slot + 1):
                    term = jnp.sum((here * power(i, g, m)).reshape(16, 8, B), axis=0)
                    totals[i] = term if totals[i] is None else totals[i] + term
            for i in range(slot + 1):
                partial[slot, i, g] = jnp.sum(totals[i], axis=0, keepdims=True)

    for slot in range(POWERS - 1):
        apply(slot)
        grams(slot)
    grams(POWERS - 1)
    gram = [
        [
            jnp.concatenate([partial[max(i, j), min(i, j), g] for g in range(2)], axis=0)
            for j in range(POWERS)
        ]
        for i in range(POWERS)
    ]
    x = tfqmr(gram, limits[...])
    for g in range(2):
        for m in range(9):
            total = x[0][g : g + 1, :] * power(0, g, m)
            for i in range(1, len(x)):
                total = total + x[i][g : g + 1, :] * power(i, g, m)
            out[g, 0, m] = total


def solve(*arrays):
    fields = [pltpu.VMEM((4 * (high - low) * B, 4 * B), BF16) for low, high in COLUMNS]
    return pl.pallas_call(
        solve_kernel,
        out_shape=jax.ShapeDtypeStruct((2, 1, 9, B, B), F32),
        in_specs=[pl.BlockSpec(memory_space=pltpu.VMEM)] * len(arrays),
        out_specs=pl.BlockSpec(memory_space=pltpu.VMEM),
        scratch_shapes=[
            pltpu.VMEM((2, 3, B, 6 * B), BF16),
            pltpu.VMEM((2, 3, B, 6 * B), BF16),
            *fields,
            *fields,
            *[pltpu.VMEM((2, 9 * B, B), F32) for _ in range(POWERS - 1)],
        ],
        compiler_params=pltpu.CompilerParams(vmem_limit_bytes=20 * 2**20),
        name="solve",
    )(*arrays)


def shift(value, axis, step):
    count = lax.axis_size(axis)
    if step > 0:
        pairs = [(i, i + 1) for i in range(count - 1)]
    else:
        pairs = [(i + 1, i) for i in range(count - 1)]
    return lax.ppermute(value, axis, pairs)


def shards(blocks, pair_mask, rhs_rows, counts):
    mask = jnp.transpose(pair_mask, (0, 1, 3, 4, 2)).reshape(-1, 9)
    sap, sam, sbp, sbm = pack(blocks, mask, rhs_rows)
    rap = shift(sap, "gy", 1)
    ram = shift(sam, "gy", -1)
    rbp = shift(sbp, "gy", 1)
    rbm = shift(sbm, "gy", -1)
    up, down = relay(mask, blocks, rhs_rows, rap, ram)
    fxp = shift(up, "gx", 1)
    fxm = shift(down, "gx", -1)
    prepared = prepare(rap, ram, rbp, rbm, mask, blocks, rhs_rows)
    orbitals = B // pair_mask.shape[-1]
    limits = jnp.repeat(counts, orbitals, axis=-1).reshape(2, B).astype(F32)
    return solve(*prepared, fxp, fxm, limits)


def solution(mesh):
    return jax.shard_map(
        shards,
        mesh=mesh,
        in_specs=(
            P("gx", "gy", None, None, None),
            P("gx", "gy", None, None, None),
            P("gx", "gy", None, None, None),
            P("gx", "gy", None),
        ),
        out_specs=P("gx", "gy", None, None, None),
        check_vma=False,
    )
```

```python
import jax
import jax.numpy as jnp
from jax import lax
from jax.experimental import pallas as pl
from jax.experimental.pallas import tpu as pltpu
from jax.sharding import PartitionSpec as P

ITERS = 3
B = 128
POWERS = 2 * ITERS + 1
F32 = jnp.float32
BF16 = jnp.bfloat16


def off(u, v):
    return 3 * (u + 1) + (v + 1)


def edge_list(v):
    low, high = min(0, v), max(0, v)
    first = []
    for row, us in ((0, (-1, 0)), (1, (0, 1))):
        first += [(row, True, off(u, w)) for u in us for w in (low, high)]
        first.append((row, False, off(-1 if row == 0 else 1, v)))
    second = []
    for row, u in ((0, 1), (1, -1)):
        second += [(row, True, off(u, w)) for w in (low, high)]
        second += [(row, False, off(0, v)), (row, False, off(u, v))]
    return first, second


def own_list(u):
    row, us = (1, (0, 1)) if u > 0 else (0, (-1, 0))
    return [(row, True, off(w, v)) for w in us for v in (-1, 0, 1)] + [(row, False, off(u, 0))]


FIRST = {v: edge_list(v)[0] for v in (1, -1)}
SECOND = {v: edge_list(v)[1] for v in (1, -1)}
OWN = {u: own_list(u) for u in (1, -1)}


PACKED = (FIRST[1], FIRST[-1], SECOND[1], SECOND[-1], OWN[1], OWN[-1])


def masked_blocks(mask, blocks):
    atoms = mask.shape[0] // 16
    orbitals = B // atoms
    lane = lax.broadcasted_iota(jnp.int32, (mask.shape[0], 2 * atoms * B), 1)
    entry = lax.broadcasted_iota(jnp.int32, (mask.shape[0], 2 * atoms * B), 0)
    select = (entry == lane // orbitals).astype(F32).astype(BF16)
    wide = lax.dot_general(
        mask[...].astype(F32).astype(BF16),
        select,
        (((0,), (0,)), ((), ())),
        preferred_element_type=F32,
    )
    for row in range(2):
        for o in range(9):
            rows = []
            for a in range(atoms):
                start = (row * atoms + a) * B
                rows.append(jnp.broadcast_to(wide[o : o + 1, start : start + B], (orbitals, B)))
            yield row, o, blocks[row, 0, o] * jnp.concatenate(rows, axis=0)


def pack_kernel(mask, blocks, rhs, *sends):
    for row, o, value in masked_blocks(mask, blocks):
        for ref, entries in zip(sends, PACKED):
            for place, listed in enumerate(entries):
                if listed == (row, True, o):
                    ref[place] = value
    for ref, entries in zip(sends, PACKED):
        for place, (row, is_coupling, o) in enumerate(entries):
            if not is_coupling:
                ref[place] = rhs[row, 0, o]


def pack(blocks, mask, rhs):
    out = [jax.ShapeDtypeStruct((len(entries), B, B), F32) for entries in PACKED]
    return pl.pallas_call(
        pack_kernel,
        out_shape=out,
        in_specs=[pl.BlockSpec(memory_space=pltpu.VMEM)] + [pl.BlockSpec(memory_space=pltpu.VMEM)] * 2,
        out_specs=[pl.BlockSpec(memory_space=pltpu.VMEM)] * 6,
        compiler_params=pltpu.CompilerParams(vmem_limit_bytes=8 * 2**20),
        name="pack",
    )(mask, blocks, rhs)


def relay_kernel(rap, ram, up, down):
    up[:5] = rap[5:]
    up[5:] = ram[5:]
    down[:5] = rap[:5]
    down[5:] = ram[:5]


def relay(rap, ram):
    return pl.pallas_call(
        relay_kernel,
        out_shape=[jax.ShapeDtypeStruct((10, B, B), F32)] * 2,
        in_specs=[pl.BlockSpec(memory_space=pltpu.VMEM)] * 2,
        out_specs=[pl.BlockSpec(memory_space=pltpu.VMEM)] * 2,
        compiler_params=pltpu.CompilerParams(vmem_limit_bytes=8 * 2**20),
        name="relay",
    )(rap, ram)


def split(value):
    high = value.astype(BF16)
    low = (value - high.astype(F32)).astype(BF16)
    return high, low


def guarded(top, bottom, floor_val):
    return top * bottom / (bottom * bottom + floor_val * floor_val)


def poly_add(left, scale, right):
    out = []
    for i in range(max(len(left), len(right))):
        if i >= len(right):
            out.append(left[i])
        elif i >= len(left):
            out.append(scale * right[i])
        else:
            out.append(left[i] + scale * right[i])
    return out


def poly_apply(p):
    return poly_add(list(p), -1.0, [jnp.zeros_like(p[0])] + list(p))


def poly_first(gram, p):
    total = p[0] * gram[0][0]
    for i in range(1, len(p)):
        total = total + p[i] * gram[0][i]
    return total


def poly_norm(gram, p):
    total = 0.0
    for i in range(len(p)):
        inner = p[i] * gram[i][i]
        for j in range(i):
            inner = inner + 2.0 * (p[j] * gram[j][i])
        total = total + p[i] * inner
    return total


def tfqmr(gram, limits):
    one = jnp.ones_like(limits)
    zero = jnp.zeros_like(limits)
    norm = gram[0][0]
    w = [one]
    y1 = [one]
    u1 = poly_apply(y1)
    v = u1
    d = [zero]
    x = [zero]
    rho, floor_val, tau = norm, 0.1 * norm, jnp.sqrt(norm)
    theta = zero
    eta = zero
    y2 = None
    u2 = None
    ww = norm
    for iteration in range(ITERS):
        if iteration > 0:
            rho_next = poly_first(gram, w)
            beta = guarded(rho_next, rho, floor_val)
            floor_val = 0.1 * jnp.sqrt(norm * ww)
            rho = rho_next
            y1 = poly_add(w, beta, y2)
            u1 = poly_apply(y1)
            v = poly_add(u1, beta, poly_add(u2, beta, v))
        alpha_floor = 0.1 * jnp.sqrt(norm * (poly_norm(gram, v) + 1e-06))
        alpha = guarded(rho, poly_first(gram, v), alpha_floor)
        ratio = guarded(1.0, alpha, 0.1)
        y2 = poly_add(y1, -alpha, v)
        u2 = poly_apply(y2)
        active = (limits > iteration).astype(F32)
        for y, u in ((y1, u1), (y2, u2)):
            w = poly_add(w, -alpha, u)
            d = poly_add(y, theta * theta * eta * ratio, d)
            ww = poly_norm(gram, w)
            theta = jnp.sqrt(ww) / tau
            cosine = 1.0 / jnp.sqrt(1.0 + theta * theta)
            tau = tau * theta * cosine
            eta = cosine * cosine * alpha
            x = poly_add(x, active * eta, d)
    return x


COLUMNS = ((0, 2), (0, 3), (1, 3))
ROWS = ((0, 2), (0, 3), (1, 4), (2, 4))


def coupling_lanes(h, c, o):
    source_row, source_col = h + o // 3 - 1, c + o % 3 - 1
    c_low, c_high = COLUMNS[c]
    place = (source_row - ROWS[h][0]) * (c_high - c_low) + source_col - c_low
    return slice(place * B, (place + 1) * B)


def prepare_kernel(rap, ram, rbp, rbm, above, mask, blocks, rhs, middle_h, middle_l, start):
    def put(h, c, is_coupling, o, value):
        if is_coupling:
            high, low = split(value)
            lanes = coupling_lanes(h, c, o)
            middle_h[h - 1, c, :, lanes] = high
            middle_l[h - 1, c, :, lanes] = low
        else:
            g = h + o // 3 - 2
            if 0 <= g <= 1:
                start[g, 3 * (h - g) + c] = value

    start[0, 1] = above[0]
    start[1, 7] = above[1]
    for v, ref_a, ref_b in ((1, rap, rbp), (-1, ram, rbm)):
        for ref, entries in ((ref_a, FIRST[v]), (ref_b, SECOND[v])):
            for place, (row, is_coupling, o) in enumerate(entries):
                put(row + 1, 1 - v, is_coupling, o, ref[place])
    for row, o, value in masked_blocks(mask, blocks):
        put(row + 1, 1, True, o, value)
    for row, u in ((0, 0), (1, 0), (0, 1), (1, -1)):
        put(row + 1, 1, False, off(u, 0), rhs[row, 0, off(u, 0)])


def outer_kernel(rxp, rxm, outer_h, outer_l, right):
    for u, ref in ((1, rxp), (-1, rxm)):
        h = 0 if u > 0 else 3
        for place, (row, is_coupling, o) in enumerate(OWN[u]):
            if is_coupling:
                high, low = split(ref[place])
                outer_h[h // 3, :, coupling_lanes(h, 1, o)] = high
                outer_l[h // 3, :, coupling_lanes(h, 1, o)] = low
            else:
                right[h // 3] = ref[place]


def outer(*arrays):
    shapes = [((2, B, 6 * B), BF16)] * 2 + [((2, B, B), F32)]
    return pl.pallas_call(
        outer_kernel,
        out_shape=[jax.ShapeDtypeStruct(*shape) for shape in shapes],
        in_specs=[pl.BlockSpec(memory_space=pltpu.VMEM)] * len(arrays),
        out_specs=[pl.BlockSpec(memory_space=pltpu.VMEM)] * len(shapes),
        compiler_params=pltpu.CompilerParams(vmem_limit_bytes=8 * 2**20),
        cost_estimate=pl.CostEstimate(flops=10**9, bytes_accessed=10**6, transcendentals=0),
        name="outer",
    )(*arrays)


def prepare(*arrays):
    shapes = [((2, 3, B, 9 * B), BF16)] * 2 + [((2, 9, B, B), F32)]
    return pl.pallas_call(
        prepare_kernel,
        out_shape=[jax.ShapeDtypeStruct(*shape) for shape in shapes],
        in_specs=[pl.BlockSpec(memory_space=pltpu.VMEM)] * len(arrays),
        out_specs=[pl.BlockSpec(memory_space=pltpu.VMEM)] * len(shapes),
        compiler_params=pltpu.CompilerParams(vmem_limit_bytes=12 * 2**20),
        cost_estimate=pl.CostEstimate(flops=10**12, bytes_accessed=10**9, transcendentals=10**9),
        name="prepare",
    )(*arrays)


def solve_kernel(
    middle_h, middle_l, outer_h, outer_l, start, fxp, fxm, limits, out, corner_h, corner_l, *scratch
):
    fields = (scratch[0:3], scratch[3:6])
    later = scratch[6:]
    corners = {}
    for u, ref in ((1, fxp), (-1, fxm)):
        part = 5 if u > 0 else 0
        for side, v in ((0, 1), (1, -1)):
            for place in range(5):
                corners[0 if u > 0 else 3, 1 - v, *FIRST[v][part + place][1:]] = (ref, side * 5 + place)

    def power(slot, g, m):
        if slot > 0:
            return later[slot - 1][g, m * B : (m + 1) * B, :]
        h, c = g + m // 3, m % 3
        found = corners.get((h, c, False, off(1 - m // 3, 1 - c)))
        if found is not None and h in (0, 3):
            return found[0][found[1]]
        return start[g, m]

    def put_field(slot, g, h, c, value):
        high, low = split(value)
        for target in range(3):
            c_low, c_high = COLUMNS[target]
            if c_low <= c < c_high:
                first = (h * (c_high - c_low) + c - c_low) * B
                ref = fields[slot % 2][target]
                ref[first : first + B, (1 + g) * B : (2 + g) * B] = high
                ref[first : first + B, 3 * g * B : (3 * g + 1) * B] = low

    def put_vector(slot, g, h, c, value):
        m = 3 * (h - g) + c
        later[slot - 1][g, m * B : (m + 1) * B, :] = value
        if slot < POWERS - 1:
            put_field(slot, g, h, c, value)

    for (h, c, is_coupling, o), (ref, place) in corners.items():
        if is_coupling:
            high, low = split(ref[place])
            corner_h[h // 3, c // 2, :, coupling_lanes(h, c, o)] = high
            corner_l[h // 3, c // 2, :, coupling_lanes(h, c, o)] = low
    for g in range(2):
        for m in range(9):
            put_field(0, g, g + m // 3, m % 3, power(0, g, m))

    def weights(h, c):
        if h in (1, 2):
            return middle_h.at[h - 1, c], middle_l.at[h - 1, c]
        if c == 1:
            return outer_h.at[h // 3], outer_l.at[h // 3]
        return corner_h.at[h // 3, c // 2], corner_l.at[h // 3, c // 2]

    def apply(slot):
        for h in range(4):
            for c in range(3):
                field = fields[slot % 2][c]
                count = COLUMNS[c][1] - COLUMNS[c][0]
                first = ROWS[h][0]
                wh, wl = weights(h, c)

                def product(weight, low, high, lanes_low, lanes_high):
                    left = weight[:, (low - first) * count * B : (high - first) * count * B]
                    right = field[low * count * B : high * count * B, lanes_low * B : lanes_high * B]
                    return jnp.dot(left, right, preferred_element_type=F32)

                values = {}
                for g in range(2):
                    if 0 <= h - g <= 2:
                        low, high = max(ROWS[h][0], g), min(ROWS[h][1], g + 3)
                        both = product(wh, low, high, 2 * g, 2 * g + 2)
                        values[g] = both[:, :B] + both[:, B:]
                if len(values) == 2:
                    both = product(wl, 1, 3, 1, 3)
                    values[0] = values[0] + both[:, :B]
                    values[1] = values[1] + both[:, B:]
                    g, other = (0, 0) if h == 1 else (1, 3)
                    values[g] = values[g] + product(wl, other, other + 1, 1 + g, 2 + g)
                else:
                    for g in values:
                        values[g] = values[g] + product(wl, *ROWS[h], 1 + g, 2 + g)
                for g in values:
                    put_vector(slot + 1, g, h, c, values[g])

    partial = {}

    def grams(slot):
        for g in range(2):
            totals = [None] * (slot + 1)
            for m in range(9):
                here = power(slot, g, m)
                for i in range(slot + 1):
                    term = jnp.sum((here * power(i, g, m)).reshape(16, 8, B), axis=0)
                    totals[i] = term if totals[i] is None else totals[i] + term
            for i in range(slot + 1):
                partial[slot, i, g] = jnp.sum(totals[i], axis=0, keepdims=True)

    for slot in range(POWERS - 1):
        apply(slot)
        grams(slot)
    grams(POWERS - 1)
    gram = [
        [
            jnp.concatenate([partial[max(i, j), min(i, j), g] for g in range(2)], axis=0)
            for j in range(POWERS)
        ]
        for i in range(POWERS)
    ]
    x = tfqmr(gram, limits[...])
    for g in range(2):
        for m in range(9):
            total = x[0][g : g + 1, :] * power(0, g, m)
            for i in range(1, len(x)):
                total = total + x[i][g : g + 1, :] * power(i, g, m)
            out[g, 0, m] = total


def solve(*arrays):
    fields = [pltpu.VMEM((4 * (high - low) * B, 4 * B), BF16) for low, high in COLUMNS]
    return pl.pallas_call(
        solve_kernel,
        out_shape=jax.ShapeDtypeStruct((2, 1, 9, B, B), F32),
        in_specs=[pl.BlockSpec(memory_space=pltpu.VMEM)] * len(arrays),
        out_specs=pl.BlockSpec(memory_space=pltpu.VMEM),
        scratch_shapes=[
            pltpu.VMEM((2, 2, B, 4 * B), BF16),
            pltpu.VMEM((2, 2, B, 4 * B), BF16),
            *fields,
            *fields,
            *[pltpu.VMEM((2, 9 * B, B), F32) for _ in range(POWERS - 1)],
        ],
        compiler_params=pltpu.CompilerParams(vmem_limit_bytes=20 * 2**20),
        name="solve",
    )(*arrays)


def shift(value, axis, step):
    count = lax.axis_size(axis)
    if step > 0:
        pairs = [(i, i + 1) for i in range(count - 1)]
    else:
        pairs = [(i + 1, i) for i in range(count - 1)]
    return lax.ppermute(value, axis, pairs)


def shards(blocks, pair_mask, rhs_rows, counts):
    mask = jnp.transpose(pair_mask, (0, 1, 3, 4, 2)).reshape(-1, 9)
    sap, sam, sbp, sbm, oxp, oxm = pack(blocks, mask, rhs_rows)
    rap = shift(sap, "gy", 1)
    ram = shift(sam, "gy", -1)
    rxp = shift(oxp, "gx", 1)
    rxm = shift(oxm, "gx", -1)
    rbp = shift(sbp, "gy", 1)
    rbm = shift(sbm, "gy", -1)
    up, down = relay(rap, ram)
    fxp = shift(up, "gx", 1)
    fxm = shift(down, "gx", -1)
    outer_h, outer_l, above = outer(rxp, rxm)
    middle_h, middle_l, start = prepare(rap, ram, rbp, rbm, above, mask, blocks, rhs_rows)
    orbitals = B // pair_mask.shape[-1]
    limits = jnp.repeat(counts, orbitals, axis=-1).reshape(2, B).astype(F32)
    return solve(middle_h, middle_l, outer_h, outer_l, start, fxp, fxm, limits)


def solution(mesh):
    return jax.shard_map(
        shards,
        mesh=mesh,
        in_specs=(
            P("gx", "gy", None, None, None),
            P("gx", "gy", None, None, None),
            P("gx", "gy", None, None, None),
            P("gx", "gy", None),
        ),
        out_specs=P("gx", "gy", None, None, None),
        check_vma=False,
    )
```

```python
import jax
import jax.numpy as jnp
from jax import lax
from jax.experimental import pallas as pl
from jax.experimental.pallas import tpu as pltpu
from jax.sharding import PartitionSpec as P

ITERS = 3
B = 128
POWERS = 2 * ITERS + 1
EXACT = 3
F32 = jnp.float32
BF16 = jnp.bfloat16


def off(u, v):
    return 3 * (u + 1) + (v + 1)


def edge_list(v):
    low, high = min(0, v), max(0, v)
    first = []
    for row, us in ((0, (-1, 0)), (1, (0, 1))):
        first += [(row, True, off(u, w)) for u in us for w in (low, high)]
        first.append((row, False, off(-1 if row == 0 else 1, v)))
    second = []
    for row, u in ((0, 1), (1, -1)):
        second += [(row, True, off(u, w)) for w in (low, high)]
        second += [(row, False, off(0, v)), (row, False, off(u, v))]
    return first, second


def own_list(u):
    row, us = (1, (0, 1)) if u > 0 else (0, (-1, 0))
    return [(row, True, off(w, v)) for w in us for v in (-1, 0, 1)] + [(row, False, off(u, 0))]


FIRST = {v: edge_list(v)[0] for v in (1, -1)}
SECOND = {v: edge_list(v)[1] for v in (1, -1)}
OWN = {u: own_list(u) for u in (1, -1)}


PACKED = (FIRST[1], FIRST[-1], SECOND[1], SECOND[-1], OWN[1], OWN[-1])


def masked_blocks(mask, blocks):
    atoms = mask.shape[0] // 16
    orbitals = B // atoms
    lane = lax.broadcasted_iota(jnp.int32, (mask.shape[0], 2 * atoms * B), 1)
    entry = lax.broadcasted_iota(jnp.int32, (mask.shape[0], 2 * atoms * B), 0)
    select = (entry == lane // orbitals).astype(F32).astype(BF16)
    wide = lax.dot_general(
        mask[...].astype(F32).astype(BF16),
        select,
        (((0,), (0,)), ((), ())),
        preferred_element_type=F32,
    )
    for row in range(2):
        for o in range(9):
            rows = []
            for a in range(atoms):
                start = (row * atoms + a) * B
                rows.append(jnp.broadcast_to(wide[o : o + 1, start : start + B], (orbitals, B)))
            yield row, o, blocks[row, 0, o] * jnp.concatenate(rows, axis=0)


def pack_kernel(mask, blocks, rhs, *sends):
    for row, o, value in masked_blocks(mask, blocks):
        for ref, entries in zip(sends, PACKED):
            for place, listed in enumerate(entries):
                if listed == (row, True, o):
                    ref[place] = value
    for ref, entries in zip(sends, PACKED):
        for place, (row, is_coupling, o) in enumerate(entries):
            if not is_coupling:
                ref[place] = rhs[row, 0, o]


def pack(blocks, mask, rhs):
    out = [jax.ShapeDtypeStruct((len(entries), B, B), F32) for entries in PACKED]
    return pl.pallas_call(
        pack_kernel,
        out_shape=out,
        in_specs=[pl.BlockSpec(memory_space=pltpu.VMEM)] + [pl.BlockSpec(memory_space=pltpu.VMEM)] * 2,
        out_specs=[pl.BlockSpec(memory_space=pltpu.VMEM)] * 6,
        compiler_params=pltpu.CompilerParams(vmem_limit_bytes=8 * 2**20),
        name="pack",
    )(mask, blocks, rhs)


def relay_kernel(rap, ram, up, down):
    up[:5] = rap[5:]
    up[5:] = ram[5:]
    down[:5] = rap[:5]
    down[5:] = ram[:5]


def relay(rap, ram):
    return pl.pallas_call(
        relay_kernel,
        out_shape=[jax.ShapeDtypeStruct((10, B, B), F32)] * 2,
        in_specs=[pl.BlockSpec(memory_space=pltpu.VMEM)] * 2,
        out_specs=[pl.BlockSpec(memory_space=pltpu.VMEM)] * 2,
        compiler_params=pltpu.CompilerParams(vmem_limit_bytes=8 * 2**20),
        name="relay",
    )(rap, ram)


def split(value):
    high = value.astype(BF16)
    low = (value - high.astype(F32)).astype(BF16)
    return high, low


def guarded(top, bottom, floor_val):
    return top * bottom / (bottom * bottom + floor_val * floor_val)


def poly_add(left, scale, right):
    out = []
    for i in range(max(len(left), len(right))):
        if i >= len(right):
            out.append(left[i])
        elif i >= len(left):
            out.append(scale * right[i])
        else:
            out.append(left[i] + scale * right[i])
    return out


def poly_apply(p):
    return poly_add(list(p), -1.0, [jnp.zeros_like(p[0])] + list(p))


def poly_first(gram, p):
    total = p[0] * gram[0][0]
    for i in range(1, len(p)):
        total = total + p[i] * gram[0][i]
    return total


def poly_norm(gram, p):
    total = 0.0
    for i in range(len(p)):
        inner = p[i] * gram[i][i]
        for j in range(i):
            inner = inner + 2.0 * (p[j] * gram[j][i])
        total = total + p[i] * inner
    return total


def tfqmr(gram, limits):
    one = jnp.ones_like(limits)
    zero = jnp.zeros_like(limits)
    norm = gram[0][0]
    w = [one]
    y1 = [one]
    u1 = poly_apply(y1)
    v = u1
    d = [zero]
    x = [zero]
    rho, floor_val, tau = norm, 0.1 * norm, jnp.sqrt(norm)
    theta = zero
    eta = zero
    y2 = None
    u2 = None
    ww = norm
    for iteration in range(ITERS):
        if iteration > 0:
            rho_next = poly_first(gram, w)
            beta = guarded(rho_next, rho, floor_val)
            floor_val = 0.1 * jnp.sqrt(norm * ww)
            rho = rho_next
            y1 = poly_add(w, beta, y2)
            u1 = poly_apply(y1)
            v = poly_add(u1, beta, poly_add(u2, beta, v))
        alpha_floor = 0.1 * jnp.sqrt(norm * (poly_norm(gram, v) + 1e-06))
        alpha = guarded(rho, poly_first(gram, v), alpha_floor)
        ratio = guarded(1.0, alpha, 0.1)
        y2 = poly_add(y1, -alpha, v)
        u2 = poly_apply(y2)
        active = (limits > iteration).astype(F32)
        for y, u in ((y1, u1), (y2, u2)):
            w = poly_add(w, -alpha, u)
            d = poly_add(y, theta * theta * eta * ratio, d)
            ww = poly_norm(gram, w)
            theta = jnp.sqrt(ww) / tau
            cosine = 1.0 / jnp.sqrt(1.0 + theta * theta)
            tau = tau * theta * cosine
            eta = cosine * cosine * alpha
            x = poly_add(x, active * eta, d)
    return x


COLUMNS = ((0, 2), (0, 3), (1, 3))
ROWS = ((0, 2), (0, 3), (1, 4), (2, 4))


def coupling_lanes(h, c, o):
    source_row, source_col = h + o // 3 - 1, c + o % 3 - 1
    c_low, c_high = COLUMNS[c]
    place = (source_row - ROWS[h][0]) * (c_high - c_low) + source_col - c_low
    return slice(place * B, (place + 1) * B)


def prepare_kernel(rap, ram, rbp, rbm, above, mask, blocks, rhs, middle_h, middle_l, start):
    def put(h, c, is_coupling, o, value):
        if is_coupling:
            high, low = split(value)
            lanes = coupling_lanes(h, c, o)
            middle_h[h - 1, c, :, lanes] = high
            middle_l[h - 1, c, :, lanes] = low
        else:
            g = h + o // 3 - 2
            if 0 <= g <= 1:
                start[g, 3 * (h - g) + c] = value

    start[0, 1] = above[0]
    start[1, 7] = above[1]
    for v, ref_a, ref_b in ((1, rap, rbp), (-1, ram, rbm)):
        for ref, entries in ((ref_a, FIRST[v]), (ref_b, SECOND[v])):
            for place, (row, is_coupling, o) in enumerate(entries):
                put(row + 1, 1 - v, is_coupling, o, ref[place])
    for row, o, value in masked_blocks(mask, blocks):
        put(row + 1, 1, True, o, value)
    for row, u in ((0, 0), (1, 0), (0, 1), (1, -1)):
        put(row + 1, 1, False, off(u, 0), rhs[row, 0, off(u, 0)])


def outer_kernel(rxp, rxm, outer_h, outer_l, right):
    for u, ref in ((1, rxp), (-1, rxm)):
        h = 0 if u > 0 else 3
        for place, (row, is_coupling, o) in enumerate(OWN[u]):
            if is_coupling:
                high, low = split(ref[place])
                outer_h[h // 3, :, coupling_lanes(h, 1, o)] = high
                outer_l[h // 3, :, coupling_lanes(h, 1, o)] = low
            else:
                right[h // 3] = ref[place]


def outer(*arrays):
    shapes = [((2, B, 6 * B), BF16)] * 2 + [((2, B, B), F32)]
    return pl.pallas_call(
        outer_kernel,
        out_shape=[jax.ShapeDtypeStruct(*shape) for shape in shapes],
        in_specs=[pl.BlockSpec(memory_space=pltpu.VMEM)] * len(arrays),
        out_specs=[pl.BlockSpec(memory_space=pltpu.VMEM)] * len(shapes),
        compiler_params=pltpu.CompilerParams(vmem_limit_bytes=8 * 2**20),
        cost_estimate=pl.CostEstimate(flops=10**9, bytes_accessed=10**6, transcendentals=0),
        name="outer",
    )(*arrays)


def prepare(*arrays):
    shapes = [((2, 3, B, 9 * B), BF16)] * 2 + [((2, 9, B, B), F32)]
    return pl.pallas_call(
        prepare_kernel,
        out_shape=[jax.ShapeDtypeStruct(*shape) for shape in shapes],
        in_specs=[pl.BlockSpec(memory_space=pltpu.VMEM)] * len(arrays),
        out_specs=[pl.BlockSpec(memory_space=pltpu.VMEM)] * len(shapes),
        compiler_params=pltpu.CompilerParams(vmem_limit_bytes=12 * 2**20),
        cost_estimate=pl.CostEstimate(flops=10**12, bytes_accessed=10**9, transcendentals=10**9),
        name="prepare",
    )(*arrays)


def solve_kernel(
    middle_h, middle_l, outer_h, outer_l, start, fxp, fxm, limits, out, corner_h, corner_l, gram_ref, *scratch
):
    fields = (scratch[0:3], scratch[3:6])
    later = scratch[6:]
    corners = {}
    for u, ref in ((1, fxp), (-1, fxm)):
        part = 5 if u > 0 else 0
        for side, v in ((0, 1), (1, -1)):
            for place in range(5):
                corners[0 if u > 0 else 3, 1 - v, *FIRST[v][part + place][1:]] = (ref, side * 5 + place)

    def power(slot, g, m):
        if slot > 0:
            return later[slot - 1][g, m * B : (m + 1) * B, :]
        h, c = g + m // 3, m % 3
        found = corners.get((h, c, False, off(1 - m // 3, 1 - c)))
        if found is not None and h in (0, 3):
            return found[0][found[1]]
        return start[g, m]

    def put_field(slot, g, h, c, value, short=False):
        high, low = split(value)
        for target in range(3):
            c_low, c_high = COLUMNS[target]
            if c_low <= c < c_high:
                first = (h * (c_high - c_low) + c - c_low) * B
                ref = fields[slot % 2][target]
                ref[first : first + B, (1 + g) * B : (2 + g) * B] = high
                if not short:
                    ref[first : first + B, 3 * g * B : (3 * g + 1) * B] = low

    def put_vector(slot, g, h, c, value, short=False):
        m = 3 * (h - g) + c
        later[slot - 1][g, m * B : (m + 1) * B, :] = value
        if slot < POWERS - 1:
            put_field(slot, g, h, c, value, short)

    for (h, c, is_coupling, o), (ref, place) in corners.items():
        if is_coupling:
            high, low = split(ref[place])
            corner_h[h // 3, c // 2, :, coupling_lanes(h, c, o)] = high
            corner_l[h // 3, c // 2, :, coupling_lanes(h, c, o)] = low
    for g in range(2):
        for m in range(9):
            put_field(0, g, g + m // 3, m % 3, power(0, g, m))

    def weights(h, c):
        if h in (1, 2):
            return middle_h.at[h - 1, c], middle_l.at[h - 1, c]
        if c == 1:
            return outer_h.at[h // 3], outer_l.at[h // 3]
        return corner_h.at[h // 3, c // 2], corner_l.at[h // 3, c // 2]

    def apply(slot, short):
        for h in range(4):
            for c in range(3):
                field = fields[slot % 2][c]
                count = COLUMNS[c][1] - COLUMNS[c][0]
                first = ROWS[h][0]
                wh, wl = weights(h, c)

                def product(weight, low, high, lanes_low, lanes_high):
                    left = weight[:, (low - first) * count * B : (high - first) * count * B]
                    right = field[low * count * B : high * count * B, lanes_low * B : lanes_high * B]
                    return jnp.dot(left, right, preferred_element_type=F32)

                values = {}
                if short:
                    if h in (1, 2):
                        both = product(wh, 1, 3, 1, 3)
                        values = {0: both[:, :B], 1: both[:, B:]}
                        g, other = (0, 0) if h == 1 else (1, 3)
                        values[g] = values[g] + product(wh, other, other + 1, 1 + g, 2 + g)
                    else:
                        g = h // 3
                        values[g] = product(wh, *ROWS[h], 1 + g, 2 + g)
                    for g in values:
                        put_vector(slot + 1, g, h, c, values[g], True)
                    continue
                for g in range(2):
                    if 0 <= h - g <= 2:
                        low, high = max(ROWS[h][0], g), min(ROWS[h][1], g + 3)
                        both = product(wh, low, high, 2 * g, 2 * g + 2)
                        values[g] = both[:, :B] + both[:, B:]
                if len(values) == 2:
                    both = product(wl, 1, 3, 1, 3)
                    values[0] = values[0] + both[:, :B]
                    values[1] = values[1] + both[:, B:]
                    g, other = (0, 0) if h == 1 else (1, 3)
                    values[g] = values[g] + product(wl, other, other + 1, 1 + g, 2 + g)
                else:
                    for g in values:
                        values[g] = values[g] + product(wl, *ROWS[h], 1 + g, 2 + g)
                for g in values:
                    put_vector(slot + 1, g, h, c, values[g])

    def grams(slot):
        for g in range(2):
            totals = [None] * (slot + 1)
            for m in range(9):
                here = power(slot, g, m)
                for i in range(slot + 1):
                    term = jnp.sum((here * power(i, g, m)).reshape(16, 8, B), axis=0)
                    totals[i] = term if totals[i] is None else totals[i] + term
            for i in range(slot + 1):
                gram_ref[slot, i, g : g + 1, :] = jnp.sum(totals[i], axis=0, keepdims=True)

    for slot in range(EXACT):
        apply(slot, False)
        grams(slot)
    size, before, first = (gram_ref[i, i] for i in (EXACT - 1, EXACT - 2, 0))
    small = jnp.logical_and(size <= 0.0256 * first, size <= 0.2 * before)
    all_small = jnp.min(small.astype(F32)) > 0.5

    def rest(short):
        for slot in range(EXACT, POWERS - 1):
            apply(slot, short)
            grams(slot)
        grams(POWERS - 1)

    pl.when(all_small)(lambda: rest(True))
    pl.when(jnp.logical_not(all_small))(lambda: rest(False))
    gram = [[gram_ref[max(i, j), min(i, j)] for j in range(POWERS)] for i in range(POWERS)]
    x = tfqmr(gram, limits[...])
    for g in range(2):
        for m in range(9):
            total = x[0][g : g + 1, :] * power(0, g, m)
            for i in range(1, len(x)):
                total = total + x[i][g : g + 1, :] * power(i, g, m)
            out[g, 0, m] = total


def solve(*arrays):
    fields = [pltpu.VMEM((4 * (high - low) * B, 4 * B), BF16) for low, high in COLUMNS]
    return pl.pallas_call(
        solve_kernel,
        out_shape=jax.ShapeDtypeStruct((2, 1, 9, B, B), F32),
        in_specs=[pl.BlockSpec(memory_space=pltpu.VMEM)] * len(arrays),
        out_specs=pl.BlockSpec(memory_space=pltpu.VMEM),
        scratch_shapes=[
            pltpu.VMEM((2, 2, B, 4 * B), BF16),
            pltpu.VMEM((2, 2, B, 4 * B), BF16),
            pltpu.VMEM((POWERS, POWERS, 2, B), F32),
            *fields,
            *fields,
            *[pltpu.VMEM((2, 9 * B, B), F32) for _ in range(POWERS - 1)],
        ],
        compiler_params=pltpu.CompilerParams(vmem_limit_bytes=20 * 2**20),
        name="solve",
    )(*arrays)


def shift(value, axis, step):
    count = lax.axis_size(axis)
    if step > 0:
        pairs = [(i, i + 1) for i in range(count - 1)]
    else:
        pairs = [(i + 1, i) for i in range(count - 1)]
    return lax.ppermute(value, axis, pairs)


def shards(blocks, pair_mask, rhs_rows, counts):
    mask = jnp.transpose(pair_mask, (0, 1, 3, 4, 2)).reshape(-1, 9)
    sap, sam, sbp, sbm, oxp, oxm = pack(blocks, mask, rhs_rows)
    rap = shift(sap, "gy", 1)
    ram = shift(sam, "gy", -1)
    rxp = shift(oxp, "gx", 1)
    rxm = shift(oxm, "gx", -1)
    rbp = shift(sbp, "gy", 1)
    rbm = shift(sbm, "gy", -1)
    up, down = relay(rap, ram)
    fxp = shift(up, "gx", 1)
    fxm = shift(down, "gx", -1)
    outer_h, outer_l, above = outer(rxp, rxm)
    middle_h, middle_l, start = prepare(rap, ram, rbp, rbm, above, mask, blocks, rhs_rows)
    orbitals = B // pair_mask.shape[-1]
    limits = jnp.repeat(counts, orbitals, axis=-1).reshape(2, B).astype(F32)
    return solve(middle_h, middle_l, outer_h, outer_l, start, fxp, fxm, limits)


def solution(mesh):
    return jax.shard_map(
        shards,
        mesh=mesh,
        in_specs=(
            P("gx", "gy", None, None, None),
            P("gx", "gy", None, None, None),
            P("gx", "gy", None, None, None),
            P("gx", "gy", None),
        ),
        out_specs=P("gx", "gy", None, None, None),
        check_vma=False,
    )
```

```python
import jax
import jax.numpy as jnp
from jax import lax
from jax.experimental import pallas as pl
from jax.experimental.pallas import tpu as pltpu
from jax.sharding import PartitionSpec as P

ITERS = 3
B = 128
POWERS = 2 * ITERS + 1
EXACT = 3
F32 = jnp.float32
BF16 = jnp.bfloat16


def off(u, v):
    return 3 * (u + 1) + (v + 1)


def edge_list(v):
    low, high = min(0, v), max(0, v)
    first = []
    for row, us in ((0, (-1, 0)), (1, (0, 1))):
        first += [(row, True, off(u, w)) for u in us for w in (low, high)]
        first.append((row, False, off(-1 if row == 0 else 1, v)))
    second = []
    for row, u in ((0, 1), (1, -1)):
        second += [(row, True, off(u, w)) for w in (low, high)]
        second += [(row, False, off(0, v)), (row, False, off(u, v))]
    return first, second


def own_list(u):
    row, us = (1, (0, 1)) if u > 0 else (0, (-1, 0))
    return [(row, True, off(w, v)) for w in us for v in (-1, 0, 1)] + [(row, False, off(u, 0))]


FIRST = {v: edge_list(v)[0] for v in (1, -1)}
SECOND = {v: edge_list(v)[1] for v in (1, -1)}
OWN = {u: own_list(u) for u in (1, -1)}


PACKED = (FIRST[1], FIRST[-1], SECOND[1], SECOND[-1], OWN[1], OWN[-1])


def masked_blocks(mask, blocks):
    atoms = mask.shape[0] // 16
    orbitals = B // atoms
    lane = lax.broadcasted_iota(jnp.int32, (mask.shape[0], 2 * atoms * B), 1)
    entry = lax.broadcasted_iota(jnp.int32, (mask.shape[0], 2 * atoms * B), 0)
    select = (entry == lane // orbitals).astype(F32).astype(BF16)
    wide = lax.dot_general(
        mask[...].astype(F32).astype(BF16),
        select,
        (((0,), (0,)), ((), ())),
        preferred_element_type=F32,
    )
    for row in range(2):
        for o in range(9):
            rows = []
            for a in range(atoms):
                start = (row * atoms + a) * B
                rows.append(jnp.broadcast_to(wide[o : o + 1, start : start + B], (orbitals, B)))
            yield row, o, blocks[row, 0, o] * jnp.concatenate(rows, axis=0)


def pack_kernel(mask, blocks, rhs, *sends):
    for row, o, value in masked_blocks(mask, blocks):
        for ref, entries in zip(sends, PACKED):
            for place, listed in enumerate(entries):
                if listed == (row, True, o):
                    ref[place] = value
    for ref, entries in zip(sends, PACKED):
        for place, (row, is_coupling, o) in enumerate(entries):
            if not is_coupling:
                ref[place] = rhs[row, 0, o]


def pack(blocks, mask, rhs):
    out = [jax.ShapeDtypeStruct((len(entries), B, B), F32) for entries in PACKED]
    return pl.pallas_call(
        pack_kernel,
        out_shape=out,
        in_specs=[pl.BlockSpec(memory_space=pltpu.VMEM)] + [pl.BlockSpec(memory_space=pltpu.VMEM)] * 2,
        out_specs=[pl.BlockSpec(memory_space=pltpu.VMEM)] * 6,
        compiler_params=pltpu.CompilerParams(vmem_limit_bytes=8 * 2**20),
        name="pack",
    )(mask, blocks, rhs)


def relay_kernel(rap, ram, up, down):
    up[:5] = rap[5:]
    up[5:] = ram[5:]
    down[:5] = rap[:5]
    down[5:] = ram[:5]


def relay(rap, ram):
    return pl.pallas_call(
        relay_kernel,
        out_shape=[jax.ShapeDtypeStruct((10, B, B), F32)] * 2,
        in_specs=[pl.BlockSpec(memory_space=pltpu.VMEM)] * 2,
        out_specs=[pl.BlockSpec(memory_space=pltpu.VMEM)] * 2,
        compiler_params=pltpu.CompilerParams(vmem_limit_bytes=8 * 2**20),
        name="relay",
    )(rap, ram)


def split(value):
    high = value.astype(BF16)
    low = (value - high.astype(F32)).astype(BF16)
    return high, low


def guarded(top, bottom, floor_val):
    return top * bottom / (bottom * bottom + floor_val * floor_val)


def poly_add(left, scale, right):
    out = []
    for i in range(max(len(left), len(right))):
        if i >= len(right):
            out.append(left[i])
        elif i >= len(left):
            out.append(scale * right[i])
        else:
            out.append(left[i] + scale * right[i])
    return out


def poly_apply(p):
    return poly_add(list(p), -1.0, [jnp.zeros_like(p[0])] + list(p))


def poly_first(gram, p):
    total = p[0] * gram[0][0]
    for i in range(1, len(p)):
        total = total + p[i] * gram[0][i]
    return total


def poly_norm(gram, p):
    total = 0.0
    for i in range(len(p)):
        inner = p[i] * gram[i][i]
        for j in range(i):
            inner = inner + 2.0 * (p[j] * gram[j][i])
        total = total + p[i] * inner
    return total


def tfqmr(gram, limits):
    one = jnp.ones_like(limits)
    zero = jnp.zeros_like(limits)
    norm = gram[0][0]
    w = [one]
    y1 = [one]
    u1 = poly_apply(y1)
    v = u1
    d = [zero]
    x = [zero]
    rho, floor_val, tau = norm, 0.1 * norm, jnp.sqrt(norm)
    theta = zero
    eta = zero
    y2 = None
    u2 = None
    ww = norm
    for iteration in range(ITERS):
        if iteration > 0:
            rho_next = poly_first(gram, w)
            beta = guarded(rho_next, rho, floor_val)
            floor_val = 0.1 * jnp.sqrt(norm * ww)
            rho = rho_next
            y1 = poly_add(w, beta, y2)
            u1 = poly_apply(y1)
            v = poly_add(u1, beta, poly_add(u2, beta, v))
        alpha_floor = 0.1 * jnp.sqrt(norm * (poly_norm(gram, v) + 1e-06))
        alpha = guarded(rho, poly_first(gram, v), alpha_floor)
        ratio = guarded(1.0, alpha, 0.1)
        y2 = poly_add(y1, -alpha, v)
        u2 = poly_apply(y2)
        active = (limits > iteration).astype(F32)
        for y, u in ((y1, u1), (y2, u2)):
            w = poly_add(w, -alpha, u)
            d = poly_add(y, theta * theta * eta * ratio, d)
            ww = poly_norm(gram, w)
            theta = jnp.sqrt(ww) / tau
            cosine = 1.0 / jnp.sqrt(1.0 + theta * theta)
            tau = tau * theta * cosine
            eta = cosine * cosine * alpha
            x = poly_add(x, active * eta, d)
    return x


COLUMNS = ((0, 2), (0, 3), (1, 3))
ROWS = ((0, 2), (0, 3), (1, 4), (2, 4))


def coupling_lanes(h, c, o):
    source_row, source_col = h + o // 3 - 1, c + o % 3 - 1
    c_low, c_high = COLUMNS[c]
    place = (source_row - ROWS[h][0]) * (c_high - c_low) + source_col - c_low
    return slice(place * B, (place + 1) * B)


def prepare_kernel(rap, ram, rbp, rbm, rxp, rxm, mask, blocks, rhs, middle_h, middle_l, outer_h, outer_l, start):
    def put(h, c, is_coupling, o, value):
        if is_coupling:
            high, low = split(value)
            lanes = coupling_lanes(h, c, o)
            if h in (1, 2):
                middle_h[h - 1, c, :, lanes] = high
                middle_l[h - 1, c, :, lanes] = low
            else:
                outer_h[h // 3, :, lanes] = high
                outer_l[h // 3, :, lanes] = low
        else:
            g = h + o // 3 - 2
            if 0 <= g <= 1:
                start[g, 3 * (h - g) + c] = value

    for v, ref_a, ref_b in ((1, rap, rbp), (-1, ram, rbm)):
        for ref, entries in ((ref_a, FIRST[v]), (ref_b, SECOND[v])):
            for place, (row, is_coupling, o) in enumerate(entries):
                put(row + 1, 1 - v, is_coupling, o, ref[place])
    for u, ref in ((1, rxp), (-1, rxm)):
        for place, (row, is_coupling, o) in enumerate(OWN[u]):
            put(0 if u > 0 else 3, 1, is_coupling, o, ref[place])
    for row, o, value in masked_blocks(mask, blocks):
        put(row + 1, 1, True, o, value)
    for row, u in ((0, 0), (1, 0), (0, 1), (1, -1)):
        put(row + 1, 1, False, off(u, 0), rhs[row, 0, off(u, 0)])


def prepare(*arrays):
    shapes = [((2, 3, B, 9 * B), BF16)] * 2 + [((2, B, 6 * B), BF16)] * 2 + [((2, 9, B, B), F32)]
    return pl.pallas_call(
        prepare_kernel,
        out_shape=[jax.ShapeDtypeStruct(*shape) for shape in shapes],
        in_specs=[pl.BlockSpec(memory_space=pltpu.VMEM)] * len(arrays),
        out_specs=[pl.BlockSpec(memory_space=pltpu.VMEM)] * len(shapes),
        compiler_params=pltpu.CompilerParams(vmem_limit_bytes=12 * 2**20),
        cost_estimate=pl.CostEstimate(flops=10**12, bytes_accessed=10**9, transcendentals=10**9),
        name="prepare",
    )(*arrays)


def solve_kernel(
    middle_h, middle_l, outer_h, outer_l, start, fxp, fxm, limits, out, corner_h, corner_l, gram_ref, *scratch
):
    fields = (scratch[0:3], scratch[3:6])
    later = scratch[6:]
    corners = {}
    for u, ref in ((1, fxp), (-1, fxm)):
        part = 5 if u > 0 else 0
        for side, v in ((0, 1), (1, -1)):
            for place in range(5):
                corners[0 if u > 0 else 3, 1 - v, *FIRST[v][part + place][1:]] = (ref, side * 5 + place)

    def power(slot, g, m):
        if slot > 0:
            return later[slot - 1][g, m * B : (m + 1) * B, :]
        h, c = g + m // 3, m % 3
        found = corners.get((h, c, False, off(1 - m // 3, 1 - c)))
        if found is not None and h in (0, 3):
            return found[0][found[1]]
        return start[g, m]

    def put_field(slot, g, h, c, value, short=False):
        high, low = split(value)
        for target in range(3):
            c_low, c_high = COLUMNS[target]
            if c_low <= c < c_high:
                first = (h * (c_high - c_low) + c - c_low) * B
                ref = fields[slot % 2][target]
                ref[first : first + B, (1 + g) * B : (2 + g) * B] = high
                if not short:
                    ref[first : first + B, 3 * g * B : (3 * g + 1) * B] = low

    def put_vector(slot, g, h, c, value, short=False):
        m = 3 * (h - g) + c
        later[slot - 1][g, m * B : (m + 1) * B, :] = value
        if slot < POWERS - 1:
            put_field(slot, g, h, c, value, short)

    for (h, c, is_coupling, o), (ref, place) in corners.items():
        if is_coupling:
            high, low = split(ref[place])
            corner_h[h // 3, c // 2, :, coupling_lanes(h, c, o)] = high
            corner_l[h // 3, c // 2, :, coupling_lanes(h, c, o)] = low
    for g in range(2):
        for m in range(9):
            put_field(0, g, g + m // 3, m % 3, power(0, g, m))

    def weights(h, c):
        if h in (1, 2):
            return middle_h.at[h - 1, c], middle_l.at[h - 1, c]
        if c == 1:
            return outer_h.at[h // 3], outer_l.at[h // 3]
        return corner_h.at[h // 3, c // 2], corner_l.at[h // 3, c // 2]

    def apply(slot, short):
        for h in range(4):
            for c in range(3):
                field = fields[slot % 2][c]
                count = COLUMNS[c][1] - COLUMNS[c][0]
                first = ROWS[h][0]
                wh, wl = weights(h, c)

                def product(weight, low, high, lanes_low, lanes_high):
                    left = weight[:, (low - first) * count * B : (high - first) * count * B]
                    right = field[low * count * B : high * count * B, lanes_low * B : lanes_high * B]
                    return jnp.dot(left, right, preferred_element_type=F32)

                values = {}
                if short:
                    if h in (1, 2):
                        both = product(wh, 1, 3, 1, 3)
                        values = {0: both[:, :B], 1: both[:, B:]}
                        g, other = (0, 0) if h == 1 else (1, 3)
                        values[g] = values[g] + product(wh, other, other + 1, 1 + g, 2 + g)
                    else:
                        g = h // 3
                        values[g] = product(wh, *ROWS[h], 1 + g, 2 + g)
                    for g in values:
                        put_vector(slot + 1, g, h, c, values[g], True)
                    continue
                for g in range(2):
                    if 0 <= h - g <= 2:
                        low, high = max(ROWS[h][0], g), min(ROWS[h][1], g + 3)
                        both = product(wh, low, high, 2 * g, 2 * g + 2)
                        values[g] = both[:, :B] + both[:, B:]
                if len(values) == 2:
                    both = product(wl, 1, 3, 1, 3)
                    values[0] = values[0] + both[:, :B]
                    values[1] = values[1] + both[:, B:]
                    g, other = (0, 0) if h == 1 else (1, 3)
                    values[g] = values[g] + product(wl, other, other + 1, 1 + g, 2 + g)
                else:
                    for g in values:
                        values[g] = values[g] + product(wl, *ROWS[h], 1 + g, 2 + g)
                for g in values:
                    put_vector(slot + 1, g, h, c, values[g])

    def grams(slot):
        for g in range(2):
            totals = [None] * (slot + 1)
            for m in range(9):
                here = power(slot, g, m)
                for i in range(slot + 1):
                    term = jnp.sum((here * power(i, g, m)).reshape(16, 8, B), axis=0)
                    totals[i] = term if totals[i] is None else totals[i] + term
            for i in range(slot + 1):
                gram_ref[slot, i, g : g + 1, :] = jnp.sum(totals[i], axis=0, keepdims=True)

    for slot in range(EXACT):
        apply(slot, False)
        grams(slot)
    size, before, first = (gram_ref[i, i] for i in (EXACT - 1, EXACT - 2, 0))
    small = jnp.logical_and(size <= 0.0256 * first, size <= 0.2 * before)
    all_small = jnp.min(small.astype(F32)) > 0.5

    def rest(short):
        for slot in range(EXACT, POWERS - 1):
            apply(slot, short)
            grams(slot)
        grams(POWERS - 1)

    pl.when(all_small)(lambda: rest(True))
    pl.when(jnp.logical_not(all_small))(lambda: rest(False))
    gram = [[gram_ref[max(i, j), min(i, j)] for j in range(POWERS)] for i in range(POWERS)]
    x = tfqmr(gram, limits[...])
    for g in range(2):
        for m in range(9):
            total = x[0][g : g + 1, :] * power(0, g, m)
            for i in range(1, len(x)):
                total = total + x[i][g : g + 1, :] * power(i, g, m)
            out[g, 0, m] = total


def solve(*arrays):
    fields = [pltpu.VMEM((4 * (high - low) * B, 4 * B), BF16) for low, high in COLUMNS]
    return pl.pallas_call(
        solve_kernel,
        out_shape=jax.ShapeDtypeStruct((2, 1, 9, B, B), F32),
        in_specs=[pl.BlockSpec(memory_space=pltpu.VMEM)] * len(arrays),
        out_specs=pl.BlockSpec(memory_space=pltpu.VMEM),
        scratch_shapes=[
            pltpu.VMEM((2, 2, B, 4 * B), BF16),
            pltpu.VMEM((2, 2, B, 4 * B), BF16),
            pltpu.VMEM((POWERS, POWERS, 2, B), F32),
            *fields,
            *fields,
            *[pltpu.VMEM((2, 9 * B, B), F32) for _ in range(POWERS - 1)],
        ],
        compiler_params=pltpu.CompilerParams(vmem_limit_bytes=20 * 2**20),
        name="solve",
    )(*arrays)


def shift(value, axis, step):
    count = lax.axis_size(axis)
    if step > 0:
        pairs = [(i, i + 1) for i in range(count - 1)]
    else:
        pairs = [(i + 1, i) for i in range(count - 1)]
    return lax.ppermute(value, axis, pairs)


def shards(blocks, pair_mask, rhs_rows, counts):
    mask = jnp.transpose(pair_mask, (0, 1, 3, 4, 2)).reshape(-1, 9)
    sap, sam, sbp, sbm, oxp, oxm = pack(blocks, mask, rhs_rows)
    rap = shift(sap, "gy", 1)
    ram = shift(sam, "gy", -1)
    rxp = shift(oxp, "gx", 1)
    rxm = shift(oxm, "gx", -1)
    rbp = shift(sbp, "gy", 1)
    rbm = shift(sbm, "gy", -1)
    up, down = relay(rap, ram)
    fxp = shift(up, "gx", 1)
    fxm = shift(down, "gx", -1)
    prepared = prepare(rap, ram, rbp, rbm, rxp, rxm, mask, blocks, rhs_rows)
    orbitals = B // pair_mask.shape[-1]
    limits = jnp.repeat(counts, orbitals, axis=-1).reshape(2, B).astype(F32)
    return solve(*prepared, fxp, fxm, limits)


def solution(mesh):
    return jax.shard_map(
        shards,
        mesh=mesh,
        in_specs=(
            P("gx", "gy", None, None, None),
            P("gx", "gy", None, None, None),
            P("gx", "gy", None, None, None),
            P("gx", "gy", None),
        ),
        out_specs=P("gx", "gy", None, None, None),
        check_vma=False,
    )
```

```python
import jax
import jax.numpy as jnp
from jax import lax
from jax.experimental import pallas as pl
from jax.experimental.pallas import tpu as pltpu
from jax.sharding import PartitionSpec as P

ITERS = 3
B = 128
POWERS = 2 * ITERS + 1
EXACT = 3
F32 = jnp.float32
BF16 = jnp.bfloat16


def off(u, v):
    return 3 * (u + 1) + (v + 1)


def edge_list(v):
    low, high = min(0, v), max(0, v)
    first = []
    for row, us in ((0, (-1, 0)), (1, (0, 1))):
        first += [(row, True, off(u, w)) for u in us for w in (low, high)]
        first.append((row, False, off(-1 if row == 0 else 1, v)))
    second = []
    for row, u in ((0, 1), (1, -1)):
        second += [(row, True, off(u, w)) for w in (low, high)]
        second += [(row, False, off(0, v)), (row, False, off(u, v))]
    return first, second


def own_list(u):
    row, us = (1, (0, 1)) if u > 0 else (0, (-1, 0))
    return [(row, True, off(w, v)) for w in us for v in (-1, 0, 1)] + [(row, False, off(u, 0))]


FIRST = {v: edge_list(v)[0] for v in (1, -1)}
SECOND = {v: edge_list(v)[1] for v in (1, -1)}
OWN = {u: own_list(u) for u in (1, -1)}


PACKED = (FIRST[1], FIRST[-1], SECOND[1], SECOND[-1], OWN[1], OWN[-1])


def masked_blocks(mask, blocks):
    atoms = mask.shape[0] // 16
    orbitals = B // atoms
    lane = lax.broadcasted_iota(jnp.int32, (mask.shape[0], 2 * atoms * B), 1)
    entry = lax.broadcasted_iota(jnp.int32, (mask.shape[0], 2 * atoms * B), 0)
    select = (entry == lane // orbitals).astype(F32).astype(BF16)
    wide = lax.dot_general(
        mask[...].astype(F32).astype(BF16),
        select,
        (((0,), (0,)), ((), ())),
        preferred_element_type=F32,
    )
    for row in range(2):
        for o in range(9):
            rows = []
            for a in range(atoms):
                start = (row * atoms + a) * B
                rows.append(jnp.broadcast_to(wide[o : o + 1, start : start + B], (orbitals, B)))
            yield row, o, blocks[row, 0, o] * jnp.concatenate(rows, axis=0)


def pack_kernel(mask, blocks, rhs, *sends):
    for row, o, value in masked_blocks(mask, blocks):
        for ref, entries in zip(sends, PACKED):
            for place, listed in enumerate(entries):
                if listed == (row, True, o):
                    ref[place] = value
    for ref, entries in zip(sends, PACKED):
        for place, (row, is_coupling, o) in enumerate(entries):
            if not is_coupling:
                ref[place] = rhs[row, 0, o]


def pack(blocks, mask, rhs):
    out = [jax.ShapeDtypeStruct((len(entries), B, B), F32) for entries in PACKED]
    return pl.pallas_call(
        pack_kernel,
        out_shape=out,
        in_specs=[pl.BlockSpec(memory_space=pltpu.VMEM)] + [pl.BlockSpec(memory_space=pltpu.VMEM)] * 2,
        out_specs=[pl.BlockSpec(memory_space=pltpu.VMEM)] * 6,
        compiler_params=pltpu.CompilerParams(vmem_limit_bytes=8 * 2**20),
        name="pack",
    )(mask, blocks, rhs)


def relay_kernel(rap, ram, up, down):
    up[:5] = rap[5:]
    up[5:] = ram[5:]
    down[:5] = rap[:5]
    down[5:] = ram[:5]


def relay(rap, ram):
    return pl.pallas_call(
        relay_kernel,
        out_shape=[jax.ShapeDtypeStruct((10, B, B), F32)] * 2,
        in_specs=[pl.BlockSpec(memory_space=pltpu.VMEM)] * 2,
        out_specs=[pl.BlockSpec(memory_space=pltpu.VMEM)] * 2,
        compiler_params=pltpu.CompilerParams(vmem_limit_bytes=8 * 2**20),
        name="relay",
    )(rap, ram)


def split(value):
    high = value.astype(BF16)
    low = (value - high.astype(F32)).astype(BF16)
    return high, low


def guarded(top, bottom, floor_val):
    return top * bottom / (bottom * bottom + floor_val * floor_val)


def poly_add(left, scale, right):
    out = []
    for i in range(max(len(left), len(right))):
        if i >= len(right):
            out.append(left[i])
        elif i >= len(left):
            out.append(scale * right[i])
        else:
            out.append(left[i] + scale * right[i])
    return out


def poly_apply(p):
    return poly_add(list(p), -1.0, [jnp.zeros_like(p[0])] + list(p))


def poly_first(gram, p):
    total = p[0] * gram[0][0]
    for i in range(1, len(p)):
        total = total + p[i] * gram[0][i]
    return total


def poly_norm(gram, p):
    total = 0.0
    for i in range(len(p)):
        inner = p[i] * gram[i][i]
        for j in range(i):
            inner = inner + 2.0 * (p[j] * gram[j][i])
        total = total + p[i] * inner
    return total


def tfqmr(gram, limits):
    one = jnp.ones_like(limits)
    zero = jnp.zeros_like(limits)
    norm = gram[0][0]
    w = [one]
    y1 = [one]
    u1 = poly_apply(y1)
    v = u1
    d = [zero]
    x = [zero]
    rho, floor_val, tau = norm, 0.1 * norm, jnp.sqrt(norm)
    theta = zero
    eta = zero
    y2 = None
    u2 = None
    ww = norm
    for iteration in range(ITERS):
        if iteration > 0:
            rho_next = poly_first(gram, w)
            beta = guarded(rho_next, rho, floor_val)
            floor_val = 0.1 * jnp.sqrt(norm * ww)
            rho = rho_next
            y1 = poly_add(w, beta, y2)
            u1 = poly_apply(y1)
            v = poly_add(u1, beta, poly_add(u2, beta, v))
        alpha_floor = 0.1 * jnp.sqrt(norm * (poly_norm(gram, v) + 1e-06))
        alpha = guarded(rho, poly_first(gram, v), alpha_floor)
        ratio = guarded(1.0, alpha, 0.1)
        y2 = poly_add(y1, -alpha, v)
        u2 = poly_apply(y2)
        active = (limits > iteration).astype(F32)
        for y, u in ((y1, u1), (y2, u2)):
            w = poly_add(w, -alpha, u)
            d = poly_add(y, theta * theta * eta * ratio, d)
            ww = poly_norm(gram, w)
            theta = jnp.sqrt(ww) / tau
            cosine = 1.0 / jnp.sqrt(1.0 + theta * theta)
            tau = tau * theta * cosine
            eta = cosine * cosine * alpha
            x = poly_add(x, active * eta, d)
    return x


COLUMNS = ((0, 2), (0, 3), (1, 3))
ROWS = ((0, 2), (0, 3), (1, 4), (2, 4))


def coupling_lanes(h, c, o):
    source_row, source_col = h + o // 3 - 1, c + o % 3 - 1
    c_low, c_high = COLUMNS[c]
    place = (source_row - ROWS[h][0]) * (c_high - c_low) + source_col - c_low
    return slice(place * B, (place + 1) * B)


def prepare_kernel(rap, ram, rbp, rbm, above, mask, blocks, rhs, middle_h, middle_l, start):
    def put(h, c, is_coupling, o, value):
        if is_coupling:
            high, low = split(value)
            lanes = coupling_lanes(h, c, o)
            middle_h[h - 1, c, :, lanes] = high
            middle_l[h - 1, c, :, lanes] = low
        else:
            g = h + o // 3 - 2
            if 0 <= g <= 1:
                start[g, 3 * (h - g) + c] = value

    start[0, 1] = above[0]
    start[1, 7] = above[1]
    for v, ref_a, ref_b in ((1, rap, rbp), (-1, ram, rbm)):
        for ref, entries in ((ref_a, FIRST[v]), (ref_b, SECOND[v])):
            for place, (row, is_coupling, o) in enumerate(entries):
                put(row + 1, 1 - v, is_coupling, o, ref[place])
    for row, o, value in masked_blocks(mask, blocks):
        put(row + 1, 1, True, o, value)
    for row, u in ((0, 0), (1, 0), (0, 1), (1, -1)):
        put(row + 1, 1, False, off(u, 0), rhs[row, 0, off(u, 0)])


def outer_kernel(rxp, rxm, outer_h, outer_l, right):
    for u, ref in ((1, rxp), (-1, rxm)):
        h = 0 if u > 0 else 3
        for place, (row, is_coupling, o) in enumerate(OWN[u]):
            if is_coupling:
                high, low = split(ref[place])
                outer_h[h // 3, :, coupling_lanes(h, 1, o)] = high
                outer_l[h // 3, :, coupling_lanes(h, 1, o)] = low
            else:
                right[h // 3] = ref[place]


def outer(*arrays):
    shapes = [((2, B, 6 * B), BF16)] * 2 + [((2, B, B), F32)]
    return pl.pallas_call(
        outer_kernel,
        out_shape=[jax.ShapeDtypeStruct(*shape) for shape in shapes],
        in_specs=[pl.BlockSpec(memory_space=pltpu.VMEM)] * len(arrays),
        out_specs=[pl.BlockSpec(memory_space=pltpu.VMEM)] * len(shapes),
        compiler_params=pltpu.CompilerParams(vmem_limit_bytes=8 * 2**20),
        cost_estimate=pl.CostEstimate(flops=0, bytes_accessed=0, transcendentals=0),
        name="outer",
    )(*arrays)


def prepare(*arrays):
    shapes = [((2, 3, B, 9 * B), BF16)] * 2 + [((2, 9, B, B), F32)]
    return pl.pallas_call(
        prepare_kernel,
        out_shape=[jax.ShapeDtypeStruct(*shape) for shape in shapes],
        in_specs=[pl.BlockSpec(memory_space=pltpu.VMEM)] * len(arrays),
        out_specs=[pl.BlockSpec(memory_space=pltpu.VMEM)] * len(shapes),
        compiler_params=pltpu.CompilerParams(vmem_limit_bytes=12 * 2**20),
        cost_estimate=pl.CostEstimate(flops=10**12, bytes_accessed=10**9, transcendentals=10**9),
        name="prepare",
    )(*arrays)


def solve_kernel(
    middle_h, middle_l, outer_h, outer_l, start, fxp, fxm, limits, out, corner_h, corner_l, gram_ref, *scratch
):
    fields = (scratch[0:3], scratch[3:6])
    later = scratch[6:]
    corners = {}
    for u, ref in ((1, fxp), (-1, fxm)):
        part = 5 if u > 0 else 0
        for side, v in ((0, 1), (1, -1)):
            for place in range(5):
                corners[0 if u > 0 else 3, 1 - v, *FIRST[v][part + place][1:]] = (ref, side * 5 + place)

    def power(slot, g, m):
        if slot > 0:
            return later[slot - 1][g, m * B : (m + 1) * B, :]
        h, c = g + m // 3, m % 3
        found = corners.get((h, c, False, off(1 - m // 3, 1 - c)))
        if found is not None and h in (0, 3):
            return found[0][found[1]]
        return start[g, m]

    def put_field(slot, g, h, c, value, short=False):
        high, low = split(value)
        for target in range(3):
            c_low, c_high = COLUMNS[target]
            if c_low <= c < c_high:
                first = (h * (c_high - c_low) + c - c_low) * B
                ref = fields[slot % 2][target]
                ref[first : first + B, (1 + g) * B : (2 + g) * B] = high
                if not short:
                    ref[first : first + B, 3 * g * B : (3 * g + 1) * B] = low

    def put_vector(slot, g, h, c, value, short=False):
        m = 3 * (h - g) + c
        later[slot - 1][g, m * B : (m + 1) * B, :] = value
        if slot < POWERS - 1:
            put_field(slot, g, h, c, value, short)

    for (h, c, is_coupling, o), (ref, place) in corners.items():
        if is_coupling:
            high, low = split(ref[place])
            corner_h[h // 3, c // 2, :, coupling_lanes(h, c, o)] = high
            corner_l[h // 3, c // 2, :, coupling_lanes(h, c, o)] = low
    for g in range(2):
        for m in range(9):
            put_field(0, g, g + m // 3, m % 3, power(0, g, m))

    def weights(h, c):
        if h in (1, 2):
            return middle_h.at[h - 1, c], middle_l.at[h - 1, c]
        if c == 1:
            return outer_h.at[h // 3], outer_l.at[h // 3]
        return corner_h.at[h // 3, c // 2], corner_l.at[h // 3, c // 2]

    def apply(slot, short):
        for h in range(4):
            for c in range(3):
                field = fields[slot % 2][c]
                count = COLUMNS[c][1] - COLUMNS[c][0]
                first = ROWS[h][0]
                wh, wl = weights(h, c)

                def product(weight, low, high, lanes_low, lanes_high):
                    left = weight[:, (low - first) * count * B : (high - first) * count * B]
                    right = field[low * count * B : high * count * B, lanes_low * B : lanes_high * B]
                    return jnp.dot(left, right, preferred_element_type=F32)

                values = {}
                if short:
                    if h in (1, 2):
                        both = product(wh, 1, 3, 1, 3)
                        values = {0: both[:, :B], 1: both[:, B:]}
                        g, other = (0, 0) if h == 1 else (1, 3)
                        values[g] = values[g] + product(wh, other, other + 1, 1 + g, 2 + g)
                    else:
                        g = h // 3
                        values[g] = product(wh, *ROWS[h], 1 + g, 2 + g)
                    for g in values:
                        put_vector(slot + 1, g, h, c, values[g], True)
                    continue
                for g in range(2):
                    if 0 <= h - g <= 2:
                        low, high = max(ROWS[h][0], g), min(ROWS[h][1], g + 3)
                        both = product(wh, low, high, 2 * g, 2 * g + 2)
                        values[g] = both[:, :B] + both[:, B:]
                if len(values) == 2:
                    both = product(wl, 1, 3, 1, 3)
                    values[0] = values[0] + both[:, :B]
                    values[1] = values[1] + both[:, B:]
                    g, other = (0, 0) if h == 1 else (1, 3)
                    values[g] = values[g] + product(wl, other, other + 1, 1 + g, 2 + g)
                else:
                    for g in values:
                        values[g] = values[g] + product(wl, *ROWS[h], 1 + g, 2 + g)
                for g in values:
                    put_vector(slot + 1, g, h, c, values[g])

    def grams(slot):
        for g in range(2):
            totals = [None] * (slot + 1)
            for m in range(9):
                here = power(slot, g, m)
                for i in range(slot + 1):
                    term = jnp.sum((here * power(i, g, m)).reshape(16, 8, B), axis=0)
                    totals[i] = term if totals[i] is None else totals[i] + term
            for i in range(slot + 1):
                gram_ref[slot, i, g : g + 1, :] = jnp.sum(totals[i], axis=0, keepdims=True)

    for slot in range(EXACT):
        apply(slot, False)
        grams(slot)
    size, before, first = (gram_ref[i, i] for i in (EXACT - 1, EXACT - 2, 0))
    small = jnp.logical_and(size <= 0.0256 * first, size <= 0.2 * before)
    all_small = jnp.min(small.astype(F32)) > 0.5

    def rest(short):
        for slot in range(EXACT, POWERS - 1):
            apply(slot, short)
            grams(slot)
        grams(POWERS - 1)

    pl.when(all_small)(lambda: rest(True))
    pl.when(jnp.logical_not(all_small))(lambda: rest(False))
    gram = [[gram_ref[max(i, j), min(i, j)] for j in range(POWERS)] for i in range(POWERS)]
    x = tfqmr(gram, limits[...])
    for g in range(2):
        for m in range(9):
            total = x[0][g : g + 1, :] * power(0, g, m)
            for i in range(1, len(x)):
                total = total + x[i][g : g + 1, :] * power(i, g, m)
            out[g, 0, m] = total


def solve(*arrays):
    fields = [pltpu.VMEM((4 * (high - low) * B, 4 * B), BF16) for low, high in COLUMNS]
    return pl.pallas_call(
        solve_kernel,
        out_shape=jax.ShapeDtypeStruct((2, 1, 9, B, B), F32),
        in_specs=[pl.BlockSpec(memory_space=pltpu.VMEM)] * len(arrays),
        out_specs=pl.BlockSpec(memory_space=pltpu.VMEM),
        scratch_shapes=[
            pltpu.VMEM((2, 2, B, 4 * B), BF16),
            pltpu.VMEM((2, 2, B, 4 * B), BF16),
            pltpu.VMEM((POWERS, POWERS, 2, B), F32),
            *fields,
            *fields,
            *[pltpu.VMEM((2, 9 * B, B), F32) for _ in range(POWERS - 1)],
        ],
        compiler_params=pltpu.CompilerParams(vmem_limit_bytes=20 * 2**20),
        name="solve",
    )(*arrays)


def shift(value, axis, step):
    count = lax.axis_size(axis)
    if step > 0:
        pairs = [(i, i + 1) for i in range(count - 1)]
    else:
        pairs = [(i + 1, i) for i in range(count - 1)]
    return lax.ppermute(value, axis, pairs)


def shards(blocks, pair_mask, rhs_rows, counts):
    mask = jnp.transpose(pair_mask, (0, 1, 3, 4, 2)).reshape(-1, 9)
    sap, sam, sbp, sbm, oxp, oxm = pack(blocks, mask, rhs_rows)
    rap = shift(sap, "gy", 1)
    ram = shift(sam, "gy", -1)
    rxp = shift(oxp, "gx", 1)
    rxm = shift(oxm, "gx", -1)
    rbp = shift(sbp, "gy", 1)
    rbm = shift(sbm, "gy", -1)
    up, down = relay(rap, ram)
    fxp = shift(up, "gx", 1)
    fxm = shift(down, "gx", -1)
    outer_h, outer_l, above = outer(rxp, rxm)
    middle_h, middle_l, start = prepare(rap, ram, rbp, rbm, above, mask, blocks, rhs_rows)
    orbitals = B // pair_mask.shape[-1]
    limits = jnp.repeat(counts, orbitals, axis=-1).reshape(2, B).astype(F32)
    return solve(middle_h, middle_l, outer_h, outer_l, start, fxp, fxm, limits)


def solution(mesh):
    return jax.shard_map(
        shards,
        mesh=mesh,
        in_specs=(
            P("gx", "gy", None, None, None),
            P("gx", "gy", None, None, None),
            P("gx", "gy", None, None, None),
            P("gx", "gy", None),
        ),
        out_specs=P("gx", "gy", None, None, None),
        check_vma=False,
    )
```
